512 devices in a mesh: walk: 32 (over z_hi, y, core), slab: 16 (over x, z_lo).
Axes of the slice: x: 4, y: 8, z: 8 (z_hi: 2, z_lo: 4; z = z_hi * 4 + z_lo), core: 2. Of those that a mesh axis runs over, the one named last changes fastest.
Arguments:
- ci_blocks: float32 [2, 3072, 4096], P(None, 'walk', 'slab'), may hold values from -6 to 6
- integrals: float32 [2, 4096, 4096], P(None, 'slab', 'walk'), as said below
- live_counts: int32 [32], P('walk'), may hold values from 24 to 96, as said below
- walk_kind: int32 [3072], P('walk'), may hold values from 0 to 2
- walk_sign: int32 [3072], P('walk'), may hold values from 0 to 1
Outputs:
- first_sigma: float32 [2, 3072, 4096], P(None, 'walk', 'slab')
- second_sigma: float32 [2, 3072, 4096], P(None, 'walk', 'slab')
The draws below stay inside these ranges and needn't reach their ends.
Inputs may be any that keep to these rules, and one draw needn't show every extreme that they name: integrals[k] is exactly symmetric for each k, every entry of magnitude under 9 / sqrt(4096). `live_counts`: some walk index has all 96 slots live in every draw.
All inputs are finite; a program needn't handle non-finite values.
Results may differ from the reference program's by a relative error of at most 0.000075.
Values sent between devices are 32-bit elements; how exact they have to be, the bound alone decides.
A program may use at most 64 MiB of HBM per device.

```python
import jax
import jax.numpy as jnp
from jax import lax

WCAP = 96
NP = 4096
WALKS = 3072
N_WALK = 32


def draw_integrals(key, part):
    key = jax.random.fold_in(key, 11)
    base = jnp.clip(jax.random.normal(key, (2, NP, NP), jnp.float32), -6.0, 6.0)
    base = base * NP ** (-0.5)
    return (base + jnp.transpose(base, (0, 2, 1))) * 0.70710678


def draw_live_counts(key, part):
    key = jax.random.fold_in(key, 23)
    first_key, second_key = jax.random.split(key)
    counts = jax.random.randint(first_key, (N_WALK,), WCAP // 4, WCAP + 1)
    where_full = jax.random.randint(second_key, (), 0, N_WALK)
    return counts.at[where_full].set(WCAP).astype(jnp.int32)


def plant(result, rng, low, high):
    extent = result.shape
    spot = [jax.random.randint(jax.random.fold_in(rng, axis), (), 0, extent[axis]) for axis in range(len(extent))]
    result = result.at[tuple(spot)].set(low)
    longest = extent.index(max(extent))
    spot[longest] = (spot[longest] + 1) % extent[longest]
    return result.at[tuple(spot)].set(high)


def block_levels(rng, extent, pieces, smallest, high):
    def one(axis_at, parts):
        draws = jax.random.uniform(jax.random.fold_in(jax.random.fold_in(rng, 6), axis_at), (parts,), jnp.float32, smallest / len(pieces), high / len(pieces))
        return jnp.repeat(jnp.exp(draws), extent[axis_at] // parts).reshape((-1,) + (1,) * (len(extent) - axis_at - 1))

    level = one(*pieces[0])
    for cut in pieces[1:]:
        level = level * one(*cut)
    return level


def normal_values(rng, shape, deviation, limit, cuts=(), kind=jnp.bfloat16):
    factor_of = block_levels(rng, shape, cuts, -0.22, 0.18) if cuts else 1.0
    entries = jax.random.normal(rng, shape, jnp.float32) * deviation * factor_of
    return jnp.minimum(jnp.maximum(entries, -limit), limit).astype(kind)


def setup_inputs(seed: int = 0) -> dict:
    key_list = jax.random.split(jax.random.key(seed), 6)
    return {
        "ci_blocks": normal_values(key_list[0], (2, WALKS, NP), 1.0, 6.0, ((1, 32), (2, 16)), jnp.float32),
        "integrals": draw_integrals(jax.random.fold_in(key_list[5], 71), 0),
        "live_counts": draw_live_counts(jax.random.fold_in(key_list[5], 71), 0),
        "walk_kind": plant(jax.random.randint(key_list[3], (WALKS,), 0, 3), jax.random.fold_in(key_list[3], 1), 0, 2).astype(jnp.int32),
        "walk_sign": plant(jax.random.randint(key_list[4], (WALKS,), 0, 2), jax.random.fold_in(key_list[4], 1), 0, 1).astype(jnp.int32),
    }


def reference(ci_blocks, integrals, live_counts, walk_kind, walk_sign):
    index = jnp.arange(WALKS, dtype=jnp.int32)
    owner = index // WCAP
    live = (index % WCAP) < live_counts[owner]
    plus_on = jnp.where(live & (walk_kind != 1), 1.0, 0.0).astype(jnp.float32)
    minus_on = jnp.where(live & (walk_kind != 0), 1.0, 0.0).astype(jnp.float32)
    minus_on = minus_on * (2 * walk_sign - 1).astype(jnp.float32)
    scale = jnp.stack([plus_on, minus_on])[:, :, None]
    first = scale * jnp.einsum("kwq,kqp->kwp", ci_blocks, integrals, precision=lax.Precision.HIGHEST)
    second = scale * jnp.einsum("kwq,kqp->kwp", first, integrals, precision=lax.Precision.HIGHEST)
    return first, second
```

```python
import functools

import jax
import jax.numpy as jnp
from jax import lax
from jax.experimental import pallas as pl
from jax.experimental.pallas import tpu as pltpu
from jax.sharding import PartitionSpec as P

MESH = pl.DeviceIdType.MESH
F32 = jnp.float32
BF16 = jnp.bfloat16


def device(x, y, z, c):
    return ((z // 4) * 16 + y * 2 + c, x * 4 + z % 4)


def split(a):
    high = a.astype(BF16)
    return high, (a - high.astype(F32)).astype(BF16)


def product(a, b, dims):
    dot = functools.partial(lax.dot_general, dimension_numbers=(dims, ((), ())), preferred_element_type=F32)
    return dot(a[0], b[0]) + (dot(a[0], b[1]) + dot(a[1], b[0]))


def kernel(
    ci, integrals, live, kind, sign, first_out, second_out,
    scaled, turned, cbuf, gbuf, part, parts_in, firsts, fold, fold_in, sums, sums_in, swap_in,
    g_send, g_recv, c_send, c_recv, mate_send, mate_recv, y_send, y_recv,
    rs_send, rs_recv, ag_send, ag_recv, fo_send, fo_recv, z_send, z_recv, sw_send, sw_recv,
):
    walk, slab = lax.axis_index("walk"), lax.axis_index("slab")
    x, zl = slab // 4, slab % 4
    zh, y, c = walk // 16, (walk // 2) % 8, walk % 2
    z = zh * 4 + zl

    def remote(src, dst, send, recv, to):
        return pltpu.make_async_remote_copy(
            src_ref=src, dst_ref=dst, send_sem=send, recv_sem=recv, device_id=to, device_id_type=MESH
        )

    def giver(quarter, k):
        return (2 * zh + c, y, (x // 2) * 4 + quarter, k)

    def is_me(place):
        return (place[0] == x) & (place[1] == y) & (place[2] == z) & (place[3] == c)

    barrier = pltpu.get_barrier_semaphore()
    near = [(x, y, (z + dz) % 8, (c + dc) % 2) for dz in range(8) for dc in range(2) if dz or dc]
    near += [(x, (y + 1) % 8, z, c), (x, (y + 7) % 8, z, c)]
    near += [((x + d) % 4, y, z, c) for d in (1, 2, 3)]
    for place in near:
        pl.semaphore_signal(barrier, inc=1, device_id=device(*place), device_id_type=MESH)
    for quarter in range(4):
        for k in range(2):
            place = giver(quarter, k)

            @pl.when(jnp.logical_not(is_me(place)))
            def _():
                pl.semaphore_signal(barrier, inc=1, device_id=device(*place), device_id_type=MESH)

    def taker(yy):
        return (2 * zh + yy // 4, y, (x // 2) * 4 + yy % 4, x % 2)

    mine = [is_me(taker(yy)) for yy in range(8)]
    own = functools.reduce(lambda a, b: a + b, [m.astype(jnp.int32) for m in mine])

    rows = lax.broadcasted_iota(jnp.int32, (96, 96), 0)
    cols = lax.broadcasted_iota(jnp.int32, (96, 96), 1)

    def column(line):
        return jnp.sum(jnp.where(rows == cols, jnp.broadcast_to(line, (96, 96)), 0.0), axis=1, keepdims=True)

    position = lax.broadcasted_iota(jnp.int32, (1, 96), 1)
    alive = position < live[...]
    plus = jnp.where(alive & (kind[...] != 1), 1.0, 0.0).astype(F32)
    minus = jnp.where(alive & (kind[...] != 0), 1.0, 0.0).astype(F32) * (2 * sign[...] - 1).astype(F32)
    scale = [column(plus), column(minus)]
    for k in range(2):
        scaled[k] = ci[k] * scale[k]
        turned[k] = integrals[k].T
    cbuf[zl, zh * 2 + c] = scaled[c]

    pl.semaphore_wait(barrier, len(near) + 8 - own)

    for e in range(2):
        for k in range(2):
            quarter = 2 * c + e
            to = (x, y, zh * 4 + quarter, k)
            src = turned.at[k, pl.ds(e * 64, 64)]
            here = is_me(to)

            @pl.when(here)
            def _():
                gbuf[zl, y] = src[...]

            @pl.when(jnp.logical_not(here))
            def _():
                remote(src, gbuf.at[zl, y], g_send.at[e, k], g_recv.at[zl], device(*to)).start()

    mate = device(x, y, z, 1 - c)
    slot = cbuf.at[zl, zh * 2 + c]
    mate_copy = remote(scaled.at[1 - c], slot, mate_send.at[0], mate_recv.at[0], mate)
    mate_copy.start()
    sent = []

    def z_step(way):
        return (z + (1 if way == 0 else 7)) % 8

    def y_step(way):
        return (y + (1 if way == 0 else 7)) % 8

    for dk in range(2):
        k = (c + dk) % 2
        for way in range(2):
            copy = remote(scaled.at[k], slot, c_send.at[way, 0, dk], c_recv.at[way, 0, dk], device(x, y, z_step(way), k))
            copy.start()
            sent.append(copy)

    def c_block(way, d, dk):
        source = (z + (8 - d if way == 0 else d)) % 8
        return cbuf.at[source % 4, (source // 4) * 2 + (c + dk) % 2]

    def y_block(way, d, rz):
        source = (y + (8 - d if way == 0 else d)) % 8
        return gbuf.at[(zl + 4 - rz) % 4, source]

    def c_copy(way, d, dk):
        block = c_block(way, d - 1, dk)
        return remote(block, block, c_send.at[way, d - 1, dk], c_recv.at[way, d - 1, dk], device(x, y, z_step(way), c))

    def c_wait(way, d, dk):
        block = c_block(way, d, dk)
        remote(block, block, c_send.at[way, d - 1, dk], c_recv.at[way, d - 1, dk], mate).wait_recv()

    def y_copy(way, d, rz):
        block = y_block(way, d - 1, rz)
        return remote(block, block, y_send.at[way, d - 1, rz], y_recv.at[way, d - 1, rz], device(x, y_step(way), z, c))

    def y_wait(way, d, rz):
        block = y_block(way, d, rz)
        remote(block, block, y_send.at[way, d - 1, rz], y_recv.at[way, d - 1, rz], mate).wait_recv()

    for rz in range(4):
        source = (zl + 4 - rz) % 4
        block = gbuf.at[source, y]
        arrived = remote(block, block, g_send.at[0, 0], g_recv.at[source], mate)
        if rz == 0:

            @pl.when(c != zl // 2)
            def _():
                arrived.wait_recv()
        else:
            arrived.wait_recv()
        for way in range(2):
            copy = y_copy(way, 1, rz)
            copy.start()
            sent.append(copy)

    for d in range(2, 5):
        for dk in range(2):
            for way in range(2):
                c_wait(way, d - 1, dk)
                if d < 4 or way == dk:
                    copy = c_copy(way, d, dk)
                    copy.start()
                    sent.append(copy)
        for rz in range(4):
            for way in range(2):
                y_wait(way, d - 1, rz)
                if d < 4 or way == rz // 2:
                    copy = y_copy(way, d, rz)
                    copy.start()
                    sent.append(copy)
    for way in range(2):
        c_wait(way, 4, way)
    mate_block = cbuf.at[zl, zh * 2 + 1 - c]
    remote(mate_block, mate_block, mate_send.at[0], mate_recv.at[0], mate).wait_recv()
    for rz in range(4):
        y_wait(rz // 2, 4, rz)

    total = None
    for s in range(4):
        a = split(cbuf[s].reshape(384, 256))
        b = split(gbuf[s].reshape(512, 256))
        one = product(a, b, ((1,), (1,)))
        total = one if total is None else total + one
    part[...] = total.reshape(4, 96, 512)

    for d in range(1, 4):
        to = (x + d) % 4
        copy = remote(part.at[to], parts_in.at[d - 1], rs_send.at[d - 1], rs_recv.at[d - 1], device(to, y, z, c))
        copy.start()
        sent.append(copy)
    for d in range(1, 4):
        remote(part.at[0], parts_in.at[d - 1], rs_send.at[d - 1], rs_recv.at[d - 1], mate).wait_recv()
    firsts[x] = (part[x] + parts_in[0]) + (parts_in[1] + parts_in[2])
    for d in range(1, 4):
        copy = remote(firsts.at[x], firsts.at[x], ag_send.at[d - 1], ag_recv.at[d - 1], device((x + d) % 4, y, z, c))
        copy.start()
        sent.append(copy)

    lane = lax.broadcasted_iota(jnp.int32, (48, 128), 1)
    for t in range(4):
        tile = firsts[x, :, pl.ds(t * 128, 128)]
        top, low = tile[:48], tile[48:]
        fold[2 * t] = jnp.where(lane < 64, top, pltpu.roll(low, 64, 1))
        fold[2 * t + 1] = jnp.where(lane < 64, pltpu.roll(top, 64, 1), low)
    for yy in range(8):

        @pl.when(mine[yy])
        def _():
            fold_in[c, zl] = fold[yy]

        @pl.when(jnp.logical_not(mine[yy]))
        def _():
            remote(fold.at[yy], fold_in.at[c, zl], fo_send.at[yy], fo_recv.at[c, zl], device(*taker(yy))).start()

    for d in range(1, 4):
        block = firsts.at[(x + 4 - d) % 4]
        remote(block, block, ag_send.at[d - 1], ag_recv.at[d - 1], mate).wait_recv()

    def second_part(target):
        a = split(firsts[pl.ds((target // 4) * 2, 2)].reshape(192, 512))
        b = split(gbuf[target % 4].reshape(512, 256))
        sums[target] = product(a, b, ((1,), (0,))).reshape(2, 96, 256)

    def target_of(way, d):
        return (z + (d if way == 0 else 8 - d)) % 8

    def z_copy(way, d, h):
        return remote(
            sums.at[target_of(way, d), h], sums_in.at[way, d - 1, h],
            z_send.at[way, d - 1, h], z_recv.at[way, d - 1, h], device(x, y, z_step(way), c),
        )

    def z_start(way, d, h):
        copy = z_copy(way, d, h)
        copy.start()
        sent.append(copy)

    def z_add(way, d, h):
        z_copy(way, d, h).wait_recv()
        target = target_of(way, d - 1)
        sums[target, h] = sums[target, h] + sums_in[way, d - 1, h]

    second_part(target_of(0, 4))
    z_start(0, 4, 0)
    z_start(1, 4, 1)
    for way in range(2):
        second_part(target_of(way, 3))
        z_start(way, 3, 1 - way)
    for d in (2, 1):
        for way in range(2):
            second_part(target_of(way, d))
    second_part(z)
    for way in range(2):
        z_add(way, 4, way)
        z_start(way, 3, way)
    for d in (3, 2):
        for half in range(2):
            for way in range(2):
                h = 1 - way if half == 0 else way
                z_add(way, d, h)
                z_start(way, d - 1, h)
    for half in range(2):
        for way in range(2):
            z_add(way, 1, 1 - way if half == 0 else way)

    copy = remote(sums.at[z, 1 - c], swap_in.at[0], sw_send.at[0], sw_recv.at[0], mate)
    copy.start()
    sent.append(copy)

    for k in range(2):
        for quarter in range(4):
            block = fold_in.at[k, quarter]

            @pl.when(jnp.logical_not(is_me(giver(quarter, k))))
            def _():
                remote(block, block, fo_send.at[0], fo_recv.at[k, quarter], mate).wait_recv()

        for t in range(2):
            left, right = fold_in[k, 2 * t], fold_in[k, 2 * t + 1]
            first_out[k, :48, t * 128 : t * 128 + 128] = jnp.where(lane < 64, left, pltpu.roll(right, 64, 1))
            first_out[k, 48:, t * 128 : t * 128 + 128] = jnp.where(lane < 64, pltpu.roll(left, 64, 1), right)

    scale_mine = jnp.where(c == 0, scale[0], scale[1])
    scale_other = jnp.where(c == 0, scale[1], scale[0])
    second_out[c] = sums[z, c] * scale_mine
    copy.wait_recv()
    second_out[1 - c] = swap_in[0] * scale_other

    for copy in sent:
        copy.wait_send()
    mate_copy.wait_send()
    for e in range(2):
        for k in range(2):

            @pl.when(jnp.logical_not(is_me((x, y, zh * 4 + 2 * c + e, k))))
            def _():
                remote(turned.at[k, pl.ds(e * 64, 64)], gbuf.at[zl, y], g_send.at[e, k], g_recv.at[0], mate).wait_send()

    for yy in range(8):

        @pl.when(jnp.logical_not(mine[yy]))
        def _():
            remote(fold.at[yy], fold_in.at[0, 0], fo_send.at[yy], fo_recv.at[0, 0], mate).wait_send()


def on_device(ci_blocks, integrals, live_counts, walk_kind, walk_sign):
    vmem = pl.BlockSpec(memory_space=pltpu.VMEM)
    dma = pltpu.SemaphoreType.DMA
    shape = jax.ShapeDtypeStruct((2, 96, 256), F32)
    return pl.pallas_call(
        kernel,
        out_shape=(shape, shape),
        in_specs=[vmem] * 5,
        out_specs=(vmem, vmem),
        scratch_shapes=[
            pltpu.VMEM((2, 96, 256), F32),
            pltpu.VMEM((2, 128, 256), F32),
            pltpu.VMEM((4, 4, 96, 256), F32),
            pltpu.VMEM((4, 8, 64, 256), F32),
            pltpu.VMEM((4, 96, 512), F32),
            pltpu.VMEM((3, 96, 512), F32),
            pltpu.VMEM((4, 96, 512), F32),
            pltpu.VMEM((8, 48, 128), F32),
            pltpu.VMEM((2, 4, 48, 128), F32),
            pltpu.VMEM((8, 2, 96, 256), F32),
            pltpu.VMEM((2, 4, 2, 96, 256), F32),
            pltpu.VMEM((1, 96, 256), F32),
            dma((2, 2)), dma((4,)),
            dma((2, 4, 2)), dma((2, 4, 2)),
            dma((1,)), dma((1,)),
            dma((2, 4, 4)), dma((2, 4, 4)),
            dma((3,)), dma((3,)),
            dma((3,)), dma((3,)),
            dma((8,)), dma((2, 4)),
            dma((2, 4, 2)), dma((2, 4, 2)),
            dma((1,)), dma((1,)),
        ],
        compiler_params=pltpu.CompilerParams(
            collective_id=0, has_side_effects=True, vmem_limit_bytes=40 << 20
        ),
        name="sigma",
    )(
        ci_blocks, integrals, live_counts.reshape(1, 1),
        walk_kind.reshape(1, 96), walk_sign.reshape(1, 96),
    )


def solution(mesh):
    placed = (P(None, "walk", "slab"), P(None, "slab", "walk"), P("walk"), P("walk"), P("walk"))
    return jax.shard_map(
        on_device,
        mesh=mesh,
        in_specs=placed,
        out_specs=(P(None, "walk", "slab"), P(None, "walk", "slab")),
        check_vma=False,
    )
```

```python
import functools

import jax
import jax.numpy as jnp
from jax import lax
from jax.experimental import pallas as pl
from jax.experimental.pallas import tpu as pltpu
from jax.sharding import PartitionSpec as P

MESH = pl.DeviceIdType.MESH
F32 = jnp.float32
BF16 = jnp.bfloat16


def device(x, y, z, c):
    return ((z // 4) * 16 + y * 2 + c, x * 4 + z % 4)


def split(a):
    high = a.astype(BF16)
    return high, (a - high.astype(F32)).astype(BF16)


def product(a, b, dims):
    dot = functools.partial(lax.dot_general, dimension_numbers=(dims, ((), ())), preferred_element_type=F32)
    return dot(a[0], b[0]) + (dot(a[0], b[1]) + dot(a[1], b[0]))


OFFSETS = (0, -1, 1, -2, 2, -3, 3, 4)
CHUNKS = ((0, 4), (4, 6), (6, 8))


def kernel(
    ci_hbm, integrals_hbm, live_hbm, kind_hbm, sign_hbm, first_out, second_out,
    ci, integrals, live, kind, sign, in_sem, scaled, turned, cbuf, gbuf, part, parts_in, firsts, fold, fold_in, sums, sums_in, swap_in,
    g_send, g_recv, c_send, c_recv, mate_send, mate_recv, y_send, y_recv,
    rs_send, rs_recv, ag_send, ag_recv, fo_send, fo_recv, z_send, z_recv, sw_send, sw_recv,
):
    loads = [
        pltpu.make_async_copy(src, dst, in_sem.at[i])
        for i, (src, dst) in enumerate(
            zip((integrals_hbm, ci_hbm, live_hbm, kind_hbm, sign_hbm), (integrals, ci, live, kind, sign))
        )
    ]
    for load in loads:
        load.start()
    walk, slab = lax.axis_index("walk"), lax.axis_index("slab")
    x, zl = slab // 4, slab % 4
    zh, y, c = walk // 16, (walk // 2) % 8, walk % 2
    z = zh * 4 + zl

    def remote(src, dst, send, recv, to):
        return pltpu.make_async_remote_copy(
            src_ref=src, dst_ref=dst, send_sem=send, recv_sem=recv, device_id=to, device_id_type=MESH
        )

    def giver(quarter, k):
        return (2 * zh + c, y, (x // 2) * 4 + quarter, k)

    def is_me(place):
        return (place[0] == x) & (place[1] == y) & (place[2] == z) & (place[3] == c)

    barrier = pltpu.get_barrier_semaphore()
    near = [(x, y, (z + dz) % 8, (c + dc) % 2) for dz in range(8) for dc in range(2) if dz or dc]
    near += [(x, (y + 1) % 8, z, c), (x, (y + 7) % 8, z, c)]
    near += [((x + d) % 4, y, z, c) for d in (1, 2, 3)]
    for place in near:
        pl.semaphore_signal(barrier, inc=1, device_id=device(*place), device_id_type=MESH)
    for quarter in range(4):
        for k in range(2):
            place = giver(quarter, k)

            @pl.when(jnp.logical_not(is_me(place)))
            def _():
                pl.semaphore_signal(barrier, inc=1, device_id=device(*place), device_id_type=MESH)

    def taker(slot):
        yy = (y + OFFSETS[slot] + 8) % 8
        return (2 * zh + yy // 4, y, (x // 2) * 4 + yy % 4, x % 2)

    mine = [is_me(taker(slot)) for slot in range(8)]
    own = functools.reduce(lambda a, b: a + b, [m.astype(jnp.int32) for m in mine])

    rows = lax.broadcasted_iota(jnp.int32, (96, 96), 0)
    cols = lax.broadcasted_iota(jnp.int32, (96, 96), 1)

    def column(line):
        return jnp.sum(jnp.where(rows == cols, jnp.broadcast_to(line, (96, 96)), 0.0), axis=1, keepdims=True)

    for load in loads:
        load.wait()
    position = lax.broadcasted_iota(jnp.int32, (1, 96), 1)
    alive = position < live[...]
    plus = jnp.where(alive & (kind[...] != 1), 1.0, 0.0).astype(F32)
    minus = jnp.where(alive & (kind[...] != 0), 1.0, 0.0).astype(F32) * (2 * sign[...] - 1).astype(F32)
    scale = [column(plus), column(minus)]
    for k in range(2):
        scaled[k] = ci[k] * scale[k]
        turned[k] = integrals[k].T
    cbuf[zl, zh * 2 + c] = scaled[c]

    pl.semaphore_wait(barrier, len(near) + 8 - own)

    for e in range(2):
        for k in range(2):
            quarter = 2 * c + e
            to = (x, y, zh * 4 + quarter, k)
            src = turned.at[k, pl.ds(e * 64, 64)]
            here = is_me(to)

            @pl.when(here)
            def _():
                gbuf[zl, 0] = src[...]

            @pl.when(jnp.logical_not(here))
            def _():
                remote(src, gbuf.at[zl, 0], g_send.at[e, k], g_recv.at[zl], device(*to)).start()

    mate = device(x, y, z, 1 - c)
    slot = cbuf.at[zl, zh * 2 + c]
    mate_copy = remote(scaled.at[1 - c], slot, mate_send.at[0], mate_recv.at[0], mate)
    mate_copy.start()
    sent = []

    def z_step(way):
        return (z + (1 if way == 0 else 7)) % 8

    def y_step(way):
        return (y + (1 if way == 0 else 7)) % 8

    for dk in range(2):
        k = (c + dk) % 2
        for way in range(2):
            copy = remote(scaled.at[k], slot, c_send.at[way, 0, dk], c_recv.at[way, 0, dk], device(x, y, z_step(way), k))
            copy.start()
            sent.append(copy)

    def c_block(way, d, dk):
        source = (z + (8 - d if way == 0 else d)) % 8
        return cbuf.at[source % 4, (source // 4) * 2 + (c + dk) % 2]

    def y_block(way, d, rz):
        slot = min(2 * d - 1 + way, 7) if d else 0
        return gbuf.at[(zl + 4 - rz) % 4, slot]

    def c_copy(way, d, dk):
        block = c_block(way, d - 1, dk)
        return remote(block, block, c_send.at[way, d - 1, dk], c_recv.at[way, d - 1, dk], device(x, y, z_step(way), c))

    def c_wait(way, d, dk):
        block = c_block(way, d, dk)
        remote(block, block, c_send.at[way, d - 1, dk], c_recv.at[way, d - 1, dk], mate).wait_recv()

    def y_copy(way, d, rz):
        return remote(y_block(way, d - 1, rz), y_block(way, d, rz), y_send.at[way, d - 1, rz], y_recv.at[way, d - 1, rz], device(x, y_step(way), z, c))

    def y_wait(way, d, rz):
        block = y_block(way, d, rz)
        remote(block, block, y_send.at[way, d - 1, rz], y_recv.at[way, d - 1, rz], mate).wait_recv()

    for rz in range(4):
        source = (zl + 4 - rz) % 4
        block = gbuf.at[source, 0]
        arrived = remote(block, block, g_send.at[0, 0], g_recv.at[source], mate)
        if rz == 0:

            @pl.when(c != zl // 2)
            def _():
                arrived.wait_recv()
        else:
            arrived.wait_recv()
        for way in range(2):
            copy = y_copy(way, 1, rz)
            copy.start()
            sent.append(copy)

    def c_round(d, dk):
        for way in range(2):
            c_wait(way, d - 1, dk)
            if d < 4 or way == dk:
                copy = c_copy(way, d, dk)
                copy.start()
                sent.append(copy)

    def y_round(d, rz):
        for way in range(2):
            y_wait(way, d - 1, rz)
            if d < 4 or way == rz // 2:
                copy = y_copy(way, d, rz)
                copy.start()
                sent.append(copy)

    for d in range(2, 5):
        for dk in range(2):
            c_round(d, dk)
            for rz in (2 * dk, 2 * dk + 1):
                y_round(d, rz)
    for way in range(2):
        c_wait(way, 4, way)
    mate_block = cbuf.at[zl, zh * 2 + 1 - c]
    remote(mate_block, mate_block, mate_send.at[0], mate_recv.at[0], mate).wait_recv()

    lanes = [pl.ds(lo * 64, (hi - lo) * 64) for lo, hi in CHUNKS]

    def first_part(lo, hi):
        total = None
        for s in range(4):
            a = split(cbuf[s].reshape(384, 256))
            b = split(gbuf[s, lo:hi].reshape((hi - lo) * 64, 256))
            one = product(a, b, ((1,), (1,)))
            total = one if total is None else total + one
        part[:, :, lo * 64 : hi * 64] = total.reshape(4, 96, (hi - lo) * 64)

    def rs_copy(i, d):
        return remote(
            part.at[(x + d) % 4, :, lanes[i]], parts_in.at[d - 1, :, lanes[i]],
            rs_send.at[i, d - 1], rs_recv.at[i, d - 1], device((x + d) % 4, y, z, c),
        )

    def ag_copy(i, d, owner):
        block = firsts.at[owner, :, lanes[i]]
        return remote(block, block, ag_send.at[i, d - 1], ag_recv.at[i, d - 1], device((x + d) % 4, y, z, c))

    def rs_start(i):
        for d in (2, 1, 3):
            copy = rs_copy(i, d)
            copy.start()
            sent.append(copy)

    def rs_end(i):
        for d in (1, 3, 2):
            rs_copy(i, d).wait_recv()
        span = lanes[i]
        firsts[x, :, span] = (part[x, :, span] + parts_in[0, :, span]) + (parts_in[1, :, span] + parts_in[2, :, span])
        for d in (2, 1, 3):
            copy = ag_copy(i, d, x)
            copy.start()
            sent.append(copy)

    def ag_end(i):
        for d in (1, 3, 2):
            ag_copy(i, d, (x + 4 - d) % 4).wait_recv()

    first_part(0, 4)
    rs_start(0)
    first_part(4, 6)
    rs_start(1)
    for rz in range(4):
        y_wait(rz // 2, 4, rz)
    first_part(6, 8)
    rs_start(2)
    for i in range(3):
        rs_end(i)

    lane = lax.broadcasted_iota(jnp.int32, (48, 128), 1)
    for t in range(4):
        tile = firsts[x, :, pl.ds(t * 128, 128)]
        top, low = tile[:48], tile[48:]
        fold[2 * t] = jnp.where(lane < 64, top, pltpu.roll(low, 64, 1))
        fold[2 * t + 1] = jnp.where(lane < 64, pltpu.roll(top, 64, 1), low)
    for yy in range(8):

        @pl.when(mine[yy])
        def _():
            fold_in[c, zl] = fold[yy]

        @pl.when(jnp.logical_not(mine[yy]))
        def _():
            remote(fold.at[yy], fold_in.at[c, zl], fo_send.at[yy], fo_recv.at[c, zl], device(*taker(yy))).start()

    for i in range(2):
        ag_end(i)
        lo, hi = CHUNKS[i]
        a = split(firsts[:, :, lanes[i]].reshape(384, (hi - lo) * 64))
        for s in range(4):
            b = split(gbuf[s, lo:hi].reshape((hi - lo) * 64, 256))
            one = product(a, b, ((1,), (0,))).reshape(4, 96, 256)
            sums[s] = one if i == 0 else sums[s] + one
    ag_end(2)

    def share(target, h):
        return sums.at[target % 4, (target // 4) * 2 + h]

    def second_part(target):
        lo, hi = CHUNKS[2]
        pair = pl.ds((target // 4) * 2, 2)
        a = split(firsts[pair, :, lanes[2]].reshape(192, (hi - lo) * 64))
        b = split(gbuf[target % 4, lo:hi].reshape((hi - lo) * 64, 256))
        sums[target % 4, pair] = sums[target % 4, pair] + product(a, b, ((1,), (0,))).reshape(2, 96, 256)

    def target_of(way, d):
        return (z + (d if way == 0 else 8 - d)) % 8

    def z_copy(way, d, h):
        return remote(
            share(target_of(way, d), h), sums_in.at[way, d - 1, h],
            z_send.at[way, d - 1, h], z_recv.at[way, d - 1, h], device(x, y, z_step(way), c),
        )

    def z_start(way, d, h):
        copy = z_copy(way, d, h)
        copy.start()
        sent.append(copy)

    def z_add(way, d, h):
        z_copy(way, d, h).wait_recv()
        mine = share(target_of(way, d - 1), h)
        mine[...] = mine[...] + sums_in[way, d - 1, h]

    second_part(target_of(0, 4))
    z_start(0, 4, 0)
    z_start(1, 4, 1)
    for way in range(2):
        second_part(target_of(way, 3))
        z_start(way, 3, 1 - way)
    for d in (2, 1):
        for way in range(2):
            second_part(target_of(way, d))
    second_part(z)
    for way in range(2):
        z_add(way, 4, way)
        z_start(way, 3, way)
    for d in (3, 2):
        for half in range(2):
            for way in range(2):
                h = 1 - way if half == 0 else way
                z_add(way, d, h)
                z_start(way, d - 1, h)
    for half in range(2):
        for way in range(2):
            z_add(way, 1, 1 - way if half == 0 else way)

    copy = remote(share(z, 1 - c), swap_in.at[0], sw_send.at[0], sw_recv.at[0], mate)
    copy.start()
    sent.append(copy)

    for k in range(2):
        for quarter in range(4):
            block = fold_in.at[k, quarter]

            @pl.when(jnp.logical_not(is_me(giver(quarter, k))))
            def _():
                remote(block, block, fo_send.at[0], fo_recv.at[k, quarter], mate).wait_recv()

        for t in range(2):
            left, right = fold_in[k, 2 * t], fold_in[k, 2 * t + 1]
            first_out[k, :48, t * 128 : t * 128 + 128] = jnp.where(lane < 64, left, pltpu.roll(right, 64, 1))
            first_out[k, 48:, t * 128 : t * 128 + 128] = jnp.where(lane < 64, pltpu.roll(left, 64, 1), right)

    scale_mine = jnp.where(c == 0, scale[0], scale[1])
    scale_other = jnp.where(c == 0, scale[1], scale[0])
    second_out[c] = share(z, c)[...] * scale_mine
    copy.wait_recv()
    second_out[1 - c] = swap_in[0] * scale_other

    for copy in sent:
        copy.wait_send()
    mate_copy.wait_send()
    for e in range(2):
        for k in range(2):

            @pl.when(jnp.logical_not(is_me((x, y, zh * 4 + 2 * c + e, k))))
            def _():
                remote(turned.at[k, pl.ds(e * 64, 64)], gbuf.at[zl, 0], g_send.at[e, k], g_recv.at[0], mate).wait_send()

    for yy in range(8):

        @pl.when(jnp.logical_not(mine[yy]))
        def _():
            remote(fold.at[yy], fold_in.at[0, 0], fo_send.at[yy], fo_recv.at[0, 0], mate).wait_send()


def on_device(ci_blocks, integrals, live_counts, walk_kind, walk_sign):
    vmem = pl.BlockSpec(memory_space=pltpu.VMEM)
    dma = pltpu.SemaphoreType.DMA
    shape = jax.ShapeDtypeStruct((2, 96, 256), F32)
    return pl.pallas_call(
        kernel,
        out_shape=(shape, shape),
        in_specs=[pl.BlockSpec(memory_space=pl.ANY)] * 5,
        out_specs=(vmem, vmem),
        scratch_shapes=[
            pltpu.VMEM((2, 96, 256), F32),
            pltpu.VMEM((2, 256, 128), F32),
            pltpu.VMEM((1, 1), jnp.int32),
            pltpu.VMEM((1, 96), jnp.int32),
            pltpu.VMEM((1, 96), jnp.int32),
            dma((5,)),
            pltpu.VMEM((2, 96, 256), F32),
            pltpu.VMEM((2, 128, 256), F32),
            pltpu.VMEM((4, 4, 96, 256), F32),
            pltpu.VMEM((4, 8, 64, 256), F32),
            pltpu.VMEM((4, 96, 512), F32),
            pltpu.VMEM((3, 96, 512), F32),
            pltpu.VMEM((4, 96, 512), F32),
            pltpu.VMEM((8, 48, 128), F32),
            pltpu.VMEM((2, 4, 48, 128), F32),
            pltpu.VMEM((4, 4, 96, 256), F32),
            pltpu.VMEM((2, 4, 2, 96, 256), F32),
            pltpu.VMEM((1, 96, 256), F32),
            dma((2, 2)), dma((4,)),
            dma((2, 4, 2)), dma((2, 4, 2)),
            dma((1,)), dma((1,)),
            dma((2, 4, 4)), dma((2, 4, 4)),
            dma((3, 3)), dma((3, 3)),
            dma((3, 3)), dma((3, 3)),
            dma((8,)), dma((2, 4)),
            dma((2, 4, 2)), dma((2, 4, 2)),
            dma((1,)), dma((1,)),
        ],
        compiler_params=pltpu.CompilerParams(
            collective_id=0, has_side_effects=True, vmem_limit_bytes=60 << 20
        ),
        name="sigma",
    )(
        ci_blocks, integrals, live_counts.reshape(1, 1),
        walk_kind.reshape(1, 96), walk_sign.reshape(1, 96),
    )


def solution(mesh):
    placed = (P(None, "walk", "slab"), P(None, "slab", "walk"), P("walk"), P("walk"), P("walk"))
    return jax.shard_map(
        on_device,
        mesh=mesh,
        in_specs=placed,
        out_specs=(P(None, "walk", "slab"), P(None, "walk", "slab")),
        check_vma=False,
    )
```

```python
import functools

import jax
import jax.numpy as jnp
from jax import lax
from jax.experimental import pallas as pl
from jax.experimental.pallas import tpu as pltpu
from jax.sharding import PartitionSpec as P

MESH = pl.DeviceIdType.MESH
F32 = jnp.float32
BF16 = jnp.bfloat16


def device(x, y, z, c):
    return ((z // 4) * 16 + y * 2 + c, x * 4 + z % 4)


def split(a):
    high = a.astype(BF16)
    return high, (a - high.astype(F32)).astype(BF16)


def product(a, b, dims):
    dot = functools.partial(lax.dot_general, dimension_numbers=(dims, ((), ())), preferred_element_type=F32)
    return dot(a[0], b[0]) + (dot(a[0], b[1]) + dot(a[1], b[0]))


OFFSETS = (0, -1, 1, -2, 2, -3, 3, 4)
UNITS = ((0, 0, 6), (0, 6, 8), (1, 0, 4), (1, 4, 8))


def kernel(
    ci_hbm, integrals_hbm, live_hbm, kind_hbm, sign_hbm, first_out, second_out,
    ci, integrals, live, kind, sign, in_sem, scaled, turned, cbuf, gbuf, part, parts_in, firsts, fold, fold_in, sums, sums_in, swap_in,
    g_send, g_recv, c_send, c_recv, mate_send, mate_recv, y_send, y_recv,
    rs_send, rs_recv, ag_send, ag_recv, fo_send, fo_recv, z_send, z_recv, sw_send, sw_recv,
):
    loads = [
        pltpu.make_async_copy(src, dst, in_sem.at[i])
        for i, (src, dst) in enumerate(
            zip((integrals_hbm, ci_hbm, live_hbm, kind_hbm, sign_hbm), (integrals, ci, live, kind, sign))
        )
    ]
    for load in loads:
        load.start()
    walk, slab = lax.axis_index("walk"), lax.axis_index("slab")
    x, zl = slab // 4, slab % 4
    zh, y, c = walk // 16, (walk // 2) % 8, walk % 2
    z = zh * 4 + zl

    def remote(src, dst, send, recv, to):
        return pltpu.make_async_remote_copy(
            src_ref=src, dst_ref=dst, send_sem=send, recv_sem=recv, device_id=to, device_id_type=MESH
        )

    givers = [(sub, quarter, k) for sub in range(2) for quarter in range(4) for k in range(2)]

    def giver(sub, quarter, k):
        return (2 * zh + sub, y, (x // 2) * 4 + quarter, k)

    def is_me(place):
        return (place[0] == x) & (place[1] == y) & (place[2] == z) & (place[3] == c)

    barrier = pltpu.get_barrier_semaphore()
    near = [(x, y, (z + dz) % 8, (c + dc) % 2) for dz in range(8) for dc in range(2) if dz or dc]
    near += [(x, (y + 1) % 8, z, c), (x, (y + 7) % 8, z, c)]
    near += [((x + d) % 4, y, z, c) for d in (1, 2, 3)]
    for place in near:
        pl.semaphore_signal(barrier, inc=1, device_id=device(*place), device_id_type=MESH)
    for which in givers:
        place = giver(*which)

        @pl.when(jnp.logical_not(is_me(place)))
        def _():
            pl.semaphore_signal(barrier, inc=1, device_id=device(*place), device_id_type=MESH)

    takers = [(h, slot) for h in range(2) for slot in range(8)]

    def taker(h, slot):
        yy = (y + OFFSETS[slot] + 8) % 8
        return (2 * zh + yy // 4, y, (x // 2) * 4 + yy % 4, c if h else 1 - c)

    mine = {which: is_me(taker(*which)) for which in takers}
    own = functools.reduce(lambda a, b: a + b, [m.astype(jnp.int32) for m in mine.values()])

    rows = lax.broadcasted_iota(jnp.int32, (96, 96), 0)
    cols = lax.broadcasted_iota(jnp.int32, (96, 96), 1)

    def column(line):
        return jnp.sum(jnp.where(rows == cols, jnp.broadcast_to(line, (96, 96)), 0.0), axis=1, keepdims=True)

    for load in loads:
        load.wait()
    position = lax.broadcasted_iota(jnp.int32, (1, 96), 1)
    alive = position < live[...]
    plus = jnp.where(alive & (kind[...] != 1), 1.0, 0.0).astype(F32)
    minus = jnp.where(alive & (kind[...] != 0), 1.0, 0.0).astype(F32) * (2 * sign[...] - 1).astype(F32)
    scale = [column(plus), column(minus)]
    for k in range(2):
        scaled[k] = ci[k] * scale[k]
        turned[k] = integrals[k].T
    cbuf[zl, 1, zh] = scaled[c]

    pl.semaphore_wait(barrier, len(near) + 16 - own)

    for e in range(2):
        for k in range(2):
            quarter = 2 * c + e
            to = (x, y, zh * 4 + quarter, k)
            src = turned.at[k, pl.ds(e * 64, 64)]
            here = is_me(to)

            @pl.when(here)
            def _():
                gbuf[zl, 0] = src[...]

            @pl.when(jnp.logical_not(here))
            def _():
                remote(src, gbuf.at[zl, 0], g_send.at[e, k], g_recv.at[zl], device(*to)).start()

    mate = device(x, y, z, 1 - c)
    mate_copy = remote(scaled.at[1 - c], cbuf.at[zl, 0, zh], mate_send.at[0], mate_recv.at[0], mate)
    mate_copy.start()
    sent = []

    def start(copy):
        copy.start()
        sent.append(copy)

    def z_step(way):
        return (z + (1 if way == 0 else 7)) % 8

    def y_step(way):
        return (y + (1 if way == 0 else 7)) % 8

    def c_first(h):
        k = c if h else 1 - c
        for way in range(2):
            start(remote(scaled.at[k], cbuf.at[zl, h, zh], c_send.at[way, 0, h], c_recv.at[way, 0, h], device(x, y, z_step(way), k)))

    def c_block(way, d, h):
        source = (z + (8 - d if way == 0 else d)) % 8
        return cbuf.at[source % 4, h, source // 4]

    def y_block(way, d, rz):
        slot = min(2 * d - 1 + way, 7) if d else 0
        return gbuf.at[(zl + 4 - rz) % 4, slot]

    def c_copy(way, d, h):
        block = c_block(way, d - 1, h)
        return remote(block, block, c_send.at[way, d - 1, h], c_recv.at[way, d - 1, h], device(x, y, z_step(way), c))

    def c_wait(way, d, h):
        block = c_block(way, d, h)
        remote(block, block, c_send.at[way, d - 1, h], c_recv.at[way, d - 1, h], mate).wait_recv()

    def y_copy(way, d, rz):
        return remote(
            y_block(way, d - 1, rz), y_block(way, d, rz),
            y_send.at[way, d - 1, rz], y_recv.at[way, d - 1, rz], device(x, y_step(way), z, c),
        )

    def y_wait(way, d, rz):
        block = y_block(way, d, rz)
        remote(block, block, y_send.at[way, d - 1, rz], y_recv.at[way, d - 1, rz], mate).wait_recv()

    def c_round(d, h):
        for way in range(2):
            c_wait(way, d - 1, h)
            if d < 4 or way == h:
                start(c_copy(way, d, h))

    def y_round(d, rz):
        for way in range(2):
            y_wait(way, d - 1, rz)
            if d < 4 or way == rz // 2:
                start(y_copy(way, d, rz))

    def y_first(rz):
        source = (zl + 4 - rz) % 4
        block = gbuf.at[source, 0]
        arrived = remote(block, block, g_send.at[0, 0], g_recv.at[source], mate)
        if rz == 0:

            @pl.when(c != zl // 2)
            def _():
                arrived.wait_recv()
        else:
            arrived.wait_recv()
        for way in range(2):
            start(y_copy(way, 1, rz))

    c_first(0)
    y_first(0)
    y_round(2, 0)
    for rz in (1, 2, 3):
        y_first(rz)
    c_round(2, 0)
    c_first(1)
    y_round(3, 0)
    for rz in (1, 2, 3):
        y_round(2, rz)
    c_round(3, 0)
    c_round(2, 1)
    y_round(4, 0)
    for rz in (1, 2, 3):
        y_round(3, rz)
    c_round(4, 0)
    c_round(3, 1)
    for rz in (1, 2, 3):
        y_round(4, rz)

    lanes = [pl.ds(lo * 64, (hi - lo) * 64) for _, lo, hi in UNITS]

    def first_part(i):
        h, lo, hi = UNITS[i]
        total = None
        for s in range(4):
            a = split(cbuf[s, h].reshape(192, 256))
            b = split(gbuf[s, lo:hi].reshape((hi - lo) * 64, 256))
            one = product(a, b, ((1,), (1,)))
            total = one if total is None else total + one
        part[h, :, :, lo * 64 : hi * 64] = total.reshape(4, 48, (hi - lo) * 64)
        for d in (2, 1, 3):
            start(rs_copy(i, d))

    def rs_copy(i, d):
        h = UNITS[i][0]
        return remote(
            part.at[h, (x + d) % 4, :, lanes[i]], parts_in.at[h, d - 1, :, lanes[i]],
            rs_send.at[i, d - 1], rs_recv.at[i, d - 1], device((x + d) % 4, y, z, c),
        )

    def ag_copy(i, d, owner):
        block = firsts.at[UNITS[i][0], owner, :, lanes[i]]
        return remote(block, block, ag_send.at[i, d - 1], ag_recv.at[i, d - 1], device((x + d) % 4, y, z, c))

    def rs_end(i):
        for d in (1, 3, 2):
            rs_copy(i, d).wait_recv()
        h, span = UNITS[i][0], lanes[i]
        firsts[h, x, :, span] = (part[h, x, :, span] + parts_in[h, 0, :, span]) + (
            parts_in[h, 1, :, span] + parts_in[h, 2, :, span]
        )
        for d in (2, 1, 3):
            start(ag_copy(i, d, x))

    def ag_end(i):
        for d in (1, 3, 2):
            ag_copy(i, d, (x + 4 - d) % 4).wait_recv()

    lane = lax.broadcasted_iota(jnp.int32, (24, 128), 1)

    def first_away(h):
        for t in range(4):
            tile = firsts[h, x, :, pl.ds(t * 128, 128)]
            top, low = tile[:24], tile[24:]
            fold[h, 2 * t] = jnp.where(lane < 64, top, pltpu.roll(low, 64, 1))
            fold[h, 2 * t + 1] = jnp.where(lane < 64, pltpu.roll(top, 64, 1), low)
        for slot in range(8):

            @pl.when(mine[h, slot])
            def _():
                fold_in[c, zl, x % 2] = fold[h, slot]

            @pl.when(jnp.logical_not(mine[h, slot]))
            def _():
                remote(
                    fold.at[h, slot], fold_in.at[c, zl, x % 2],
                    fo_send.at[h, slot], fo_recv.at[c, zl, x % 2], device(*taker(h, slot)),
                ).start()

    def target_of(way, d):
        return (z + (d if way == 0 else 8 - d)) % 8

    def second_early(i):
        h, lo, hi = UNITS[i]
        a = split(firsts[h, :, :, lanes[i]].reshape(192, (hi - lo) * 64))
        for s in range(4):
            b = split(gbuf[s, lo:hi].reshape((hi - lo) * 64, 256))
            sums[s, h] = product(a, b, ((1,), (0,))).reshape(2, 96, 256)

    def second_late(i, target):
        h, lo, hi = UNITS[i]
        a = split(firsts[h, pl.ds((target // 4) * 2, 2), :, lanes[i]].reshape(96, (hi - lo) * 64))
        b = split(gbuf[target % 4, lo:hi].reshape((hi - lo) * 64, 256))
        sums[target % 4, h, target // 4] = sums[target % 4, h, target // 4] + product(a, b, ((1,), (0,)))

    def z_copy(h, way, d, j):
        target = target_of(way, d)
        return remote(
            sums.at[target % 4, h, target // 4, pl.ds(j * 48, 48)], sums_in.at[h, way, d - 1, pl.ds(j * 48, 48)],
            z_send.at[h, way, d - 1, j], z_recv.at[h, way, d - 1, j], device(x, y, z_step(way), c),
        )

    def z_add(h, way, d, j):
        z_copy(h, way, d, j).wait_recv()
        target, rows = target_of(way, d - 1), pl.ds(j * 48, 48)
        sums[target % 4, h, target // 4, rows] = (
            sums[target % 4, h, target // 4, rows] + sums_in[h, way, d - 1, rows]
        )

    def z_begin(i):
        h = UNITS[i][0]
        long, short = (0, 1) if h == 0 else (1, 0)
        for way, d in ((long, 4), (short, 3)):
            second_late(i, target_of(way, d))
            for j in range(2):
                start(z_copy(h, way, d, j))
        for d in (3, 2, 1):
            second_late(i, target_of(long, d))
            if d < 3:
                second_late(i, target_of(short, d))
        second_late(i, z)

    def z_round(h, r):
        long, short = (0, 1) if h == 0 else (1, 0)
        for j in range(2):
            for way, d in ((long, 5 - r), (short, 4 - r)):
                if d >= 1:
                    z_add(h, way, d, j)
                    if d > 1:
                        start(z_copy(h, way, d - 1, j))

    for way in range(2):
        if way == 0:
            c_wait(way, 4, 0)
    mate_block = cbuf.at[zl, 0, zh]
    remote(mate_block, mate_block, mate_send.at[0], mate_recv.at[0], mate).wait_recv()
    first_part(0)
    c_round(4, 1)
    for rz in range(4):
        y_wait(rz // 2, 4, rz)
    first_part(1)
    c_wait(1, 4, 1)
    first_part(2)
    rs_end(0)
    rs_end(1)
    first_part(3)
    first_away(0)
    ag_end(0)
    second_early(0)
    rs_end(2)
    ag_end(1)
    z_begin(1)
    rs_end(3)
    first_away(1)
    z_round(0, 1)
    ag_end(2)
    second_early(2)
    z_round(0, 2)
    ag_end(3)
    z_begin(3)
    z_round(0, 3)
    z_round(1, 1)
    z_round(0, 4)
    swap = remote(sums.at[zl, 0, zh], swap_in.at[0], sw_send.at[0], sw_recv.at[0], mate)
    start(swap)
    z_round(1, 2)

    for which in givers:
        sub, quarter, k = which
        block = fold_in.at[k, quarter, sub]

        @pl.when(jnp.logical_not(is_me(giver(*which))))
        def _():
            remote(block, block, fo_send.at[0, 0], fo_recv.at[k, quarter, sub], mate).wait_recv()

    for k in range(2):
        for sub in range(2):
            for t in range(2):
                left, right = fold_in[k, 2 * t, sub], fold_in[k, 2 * t + 1, sub]
                rows, span = sub * 48, slice(t * 128, t * 128 + 128)
                first_out[k, rows : rows + 24, span] = jnp.where(lane < 64, left, pltpu.roll(right, 64, 1))
                first_out[k, rows + 24 : rows + 48, span] = jnp.where(lane < 64, pltpu.roll(left, 64, 1), right)

    z_round(1, 3)
    z_round(1, 4)
    scale_mine = jnp.where(c == 0, scale[0], scale[1])
    scale_other = jnp.where(c == 0, scale[1], scale[0])
    second_out[c] = sums[zl, 1, zh] * scale_mine
    swap.wait_recv()
    second_out[1 - c] = swap_in[0] * scale_other

    for copy in sent:
        copy.wait_send()
    mate_copy.wait_send()
    for e in range(2):
        for k in range(2):

            @pl.when(jnp.logical_not(is_me((x, y, zh * 4 + 2 * c + e, k))))
            def _():
                remote(turned.at[k, pl.ds(e * 64, 64)], gbuf.at[zl, 0], g_send.at[e, k], g_recv.at[0], mate).wait_send()

    for which in takers:

        @pl.when(jnp.logical_not(mine[which]))
        def _():
            remote(fold.at[which], fold_in.at[0, 0, 0], fo_send.at[which], fo_recv.at[0, 0, 0], mate).wait_send()


def on_device(ci_blocks, integrals, live_counts, walk_kind, walk_sign):
    vmem = pl.BlockSpec(memory_space=pltpu.VMEM)
    dma = pltpu.SemaphoreType.DMA
    shape = jax.ShapeDtypeStruct((2, 96, 256), F32)
    return pl.pallas_call(
        kernel,
        out_shape=(shape, shape),
        in_specs=[pl.BlockSpec(memory_space=pl.ANY)] * 5,
        out_specs=(vmem, vmem),
        scratch_shapes=[
            pltpu.VMEM((2, 96, 256), F32),
            pltpu.VMEM((2, 256, 128), F32),
            pltpu.VMEM((1, 1), jnp.int32),
            pltpu.VMEM((1, 96), jnp.int32),
            pltpu.VMEM((1, 96), jnp.int32),
            dma((5,)),
            pltpu.VMEM((2, 96, 256), F32),
            pltpu.VMEM((2, 128, 256), F32),
            pltpu.VMEM((4, 2, 2, 96, 256), F32),
            pltpu.VMEM((4, 8, 64, 256), F32),
            pltpu.VMEM((2, 4, 48, 512), F32),
            pltpu.VMEM((2, 3, 48, 512), F32),
            pltpu.VMEM((2, 4, 48, 512), F32),
            pltpu.VMEM((2, 8, 24, 128), F32),
            pltpu.VMEM((2, 4, 2, 24, 128), F32),
            pltpu.VMEM((4, 2, 2, 96, 256), F32),
            pltpu.VMEM((2, 2, 4, 96, 256), F32),
            pltpu.VMEM((1, 96, 256), F32),
            dma((2, 2)), dma((4,)),
            dma((2, 4, 2)), dma((2, 4, 2)),
            dma((1,)), dma((1,)),
            dma((2, 4, 4)), dma((2, 4, 4)),
            dma((4, 3)), dma((4, 3)),
            dma((4, 3)), dma((4, 3)),
            dma((2, 8)), dma((2, 4, 2)),
            dma((2, 2, 4, 2)), dma((2, 2, 4, 2)),
            dma((1,)), dma((1,)),
        ],
        compiler_params=pltpu.CompilerParams(
            collective_id=0, has_side_effects=True, vmem_limit_bytes=60 << 20
        ),
        name="sigma",
    )(
        ci_blocks, integrals, live_counts.reshape(1, 1),
        walk_kind.reshape(1, 96), walk_sign.reshape(1, 96),
    )


def solution(mesh):
    placed = (P(None, "walk", "slab"), P(None, "slab", "walk"), P("walk"), P("walk"), P("walk"))
    return jax.shard_map(
        on_device,
        mesh=mesh,
        in_specs=placed,
        out_specs=(P(None, "walk", "slab"), P(None, "walk", "slab")),
        check_vma=False,
    )
```

```python
import functools

import jax
import jax.numpy as jnp
from jax import lax
from jax.experimental import pallas as pl
from jax.experimental.pallas import tpu as pltpu
from jax.sharding import PartitionSpec as P

MESH = pl.DeviceIdType.MESH
F32 = jnp.float32
BF16 = jnp.bfloat16


def device(x, y, z, c):
    return ((z // 4) * 16 + y * 2 + c, x * 4 + z % 4)


def split(a):
    high = a.astype(BF16)
    return high, (a - high.astype(F32)).astype(BF16)


def product(a, b, dims):
    dot = functools.partial(lax.dot_general, dimension_numbers=(dims, ((), ())), preferred_element_type=F32)
    return dot(a[0], b[0]) + (dot(a[0], b[1]) + dot(a[1], b[0]))


OFFSETS = (0, -1, 1, -2, 2, -3, 3, 4)
UNITS = ((0, 0, 6), (0, 6, 8), (1, 0, 6), (1, 6, 8))


def kernel(
    ci_hbm, integrals_hbm, live_hbm, kind_hbm, sign_hbm, first_out, second_out,
    ci, integrals, live, kind, sign, in_sem, turned, cbuf, gbuf, part, parts_in, firsts, fold, fold_in, sums, sums_in,
    g_send, g_recv, c_send, c_recv, m_send, m_recv, y_send, y_recv,
    rs_send, rs_recv, ag_send, ag_recv, fo_send, fo_recv, z_send, z_recv,
):
    loads = [
        pltpu.make_async_copy(src, dst, in_sem.at[i])
        for i, (src, dst) in enumerate(
            zip((integrals_hbm, ci_hbm, live_hbm, kind_hbm, sign_hbm), (integrals, ci, live, kind, sign))
        )
    ]
    for load in loads:
        load.start()
    walk, slab = lax.axis_index("walk"), lax.axis_index("slab")
    x, zl = slab // 4, slab % 4
    zh, y, c = walk // 16, (walk // 2) % 8, walk % 2
    z = zh * 4 + zl

    def remote(src, dst, send, recv, to):
        return pltpu.make_async_remote_copy(
            src_ref=src, dst_ref=dst, send_sem=send, recv_sem=recv, device_id=to, device_id_type=MESH
        )

    givers = [(sub, quarter) for sub in range(2) for quarter in range(4)]

    def giver(sub, quarter):
        return (2 * zh + sub, y, (x // 2) * 4 + quarter, c)

    def is_me(place):
        return (place[0] == x) & (place[1] == y) & (place[2] == z) & (place[3] == c)

    barrier = pltpu.get_barrier_semaphore()
    near = [(x, y, (z + dz) % 8, (c + dc) % 2) for dz in range(8) for dc in range(2) if dz or dc]
    near += [(x, (y + 1) % 8, z, c), (x, (y + 7) % 8, z, c)]
    near += [((x + d) % 4, y, z, c) for d in (1, 2, 3)]
    for place in near:
        pl.semaphore_signal(barrier, inc=1, device_id=device(*place), device_id_type=MESH)
    for which in givers:
        place = giver(*which)

        @pl.when(jnp.logical_not(is_me(place)))
        def _():
            pl.semaphore_signal(barrier, inc=1, device_id=device(*place), device_id_type=MESH)

    def taker(slot):
        yy = (y + OFFSETS[slot] + 8) % 8
        return (2 * zh + yy // 4, y, (x // 2) * 4 + yy % 4, c)

    mine = [is_me(taker(slot)) for slot in range(8)]
    own = functools.reduce(lambda a, b: a + b, [m.astype(jnp.int32) for m in mine])

    rows = lax.broadcasted_iota(jnp.int32, (96, 96), 0)
    cols = lax.broadcasted_iota(jnp.int32, (96, 96), 1)

    def column(line):
        return jnp.sum(jnp.where(rows == cols, jnp.broadcast_to(line, (96, 96)), 0.0), axis=1, keepdims=True)

    for load in loads:
        load.wait()
    position = lax.broadcasted_iota(jnp.int32, (1, 96), 1)
    alive = position < live[...]
    plus = jnp.where(alive & (kind[...] != 1), 1.0, 0.0).astype(F32)
    minus = jnp.where(alive & (kind[...] != 0), 1.0, 0.0).astype(F32) * (2 * sign[...] - 1).astype(F32)
    scale = [column(plus), column(minus)]
    for k in range(2):
        cbuf[k, zl, zh] = ci[k] * scale[k]
        turned[k] = integrals[k].T

    pl.semaphore_wait(barrier, len(near) + 8 - own)

    mate = device(x, y, z, 1 - c)
    sent = []

    def start(copy):
        copy.start()
        sent.append(copy)

    def z_step(way):
        return (z + (1 if way == 0 else 7)) % 8

    def y_step(way):
        return (y + (1 if way == 0 else 7)) % 8

    pieces = [(e, half) for e in range(2) for half in range(2)]

    def quarter_of(e, half):
        return (x, y, zh * 4 + 2 * c + e, half)

    def g_copy(k, e, half):
        return remote(
            turned.at[k, pl.ds(e * 64 + half * 32, 32)], gbuf.at[k, 0, half, (2 * c + e + 4 - zl) % 4],
            g_send.at[k, e, half], g_recv.at[k, (2 * c + e + 4 - zl) % 4], device(*quarter_of(e, half)),
        )

    def g_first(k):
        for e, half in pieces:
            here = is_me(quarter_of(e, half))

            @pl.when(here)
            def _():
                gbuf[k, 0, half, 0] = turned[k, e * 64 + half * 32 : e * 64 + half * 32 + 32]

            @pl.when(jnp.logical_not(here))
            def _():
                g_copy(k, e, half).start()

    def g_wait(k, rz):
        block = gbuf.at[k, 0, c, rz]
        arrived = remote(block, block, g_send.at[k, 0, 0], g_recv.at[k, rz], mate)
        if rz == 0:

            @pl.when(c != zl // 2)
            def _():
                arrived.wait_recv()
        else:
            arrived.wait_recv()

    def c_block(k, way, d, j):
        source = (z + (8 - d if way == 0 else d)) % 8
        return cbuf.at[k, source % 4, source // 4, pl.ds(j * 48, 48)]

    def c_start(k, d):
        for j in range(2):
            for way in range(2):
                if d < 4 or way == j:
                    block = c_block(k, way, d - 1, j)
                    if d > 1:
                        c_wait(k, way, d - 1, j)
                    start(remote(
                        block, block, c_send.at[k, way, d - 1, j], c_recv.at[k, way, d - 1, j],
                        device(x, y, z_step(way), c),
                    ))
                else:
                    c_wait(k, way, d - 1, j)

    def c_wait(k, way, d, j):
        block = c_block(k, way, d, j)
        remote(block, block, c_send.at[k, way, d - 1, j], c_recv.at[k, way, d - 1, j], mate).wait_recv()

    def y_block(k, way, d, rz):
        slot = min(2 * d - 1 + way, 7) if d else 0
        return gbuf.at[k, slot, c, rz]

    def y_wait(k, way, d, rz):
        block = y_block(k, way, d, rz)
        remote(block, block, y_send.at[k, way, d - 1, rz], y_recv.at[k, way, d - 1, rz], mate).wait_recv()

    def y_start(k, d, *chunks):
        for rz in chunks:
            if d == 1:
                g_wait(k, rz)
            for way in range(2):
                if d > 1:
                    y_wait(k, way, d - 1, rz)
                if d < 4 or way == rz // 2:
                    start(remote(
                        y_block(k, way, d - 1, rz), y_block(k, way, d, rz),
                        y_send.at[k, way, d - 1, rz], y_recv.at[k, way, d - 1, rz], device(x, y_step(way), z, c),
                    ))
        if chunks[-1] == 3:
            for slot in (0,) if d == 1 else (2 * d - 3, 2 * d - 2):
                m_start(k, slot)

    def y_end(k):
        for rz in range(4):
            y_wait(k, rz // 2, 4, rz)
        m_start(k, 7)

    def m_start(k, slot):
        block = gbuf.at[k, slot, c]
        start(remote(block, block, m_send.at[k, slot], m_recv.at[k, slot], mate))

    def m_end(k, lo, hi):
        for slot in range(lo, hi):
            block = gbuf.at[k, slot, 1 - c]
            remote(block, block, m_send.at[k, slot], m_recv.at[k, slot], mate).wait_recv()

    lanes = [pl.ds(lo * 64, (hi - lo) * 64) for _, lo, hi in UNITS]

    def g_tile(k, lo, hi, rz):
        return split(gbuf[k, lo:hi, :, rz].reshape((hi - lo) * 64, 256))

    def first_part(i):
        k, lo, hi = UNITS[i]
        m_end(k, lo, hi)
        total = None
        for rz in range(4):
            a = split(cbuf[k, (zl + 4 - rz) % 4].reshape(192, 256))
            one = product(a, g_tile(k, lo, hi, rz), ((1,), (1,)))
            total = one if total is None else total + one
        part[k, :, :, lo * 64 : hi * 64] = total.reshape(4, 48, (hi - lo) * 64)
        for d in (2, 1, 3):
            start(rs_copy(i, d))

    def rs_copy(i, d):
        h = UNITS[i][0]
        return remote(
            part.at[h, (x + d) % 4, :, lanes[i]], parts_in.at[h, d - 1, :, lanes[i]],
            rs_send.at[i, d - 1], rs_recv.at[i, d - 1], device((x + d) % 4, y, z, c),
        )

    def ag_copy(i, d, owner):
        block = firsts.at[UNITS[i][0], owner, :, lanes[i]]
        return remote(block, block, ag_send.at[i, d - 1], ag_recv.at[i, d - 1], device((x + d) % 4, y, z, c))

    def rs_end(i):
        for d in (1, 3, 2):
            rs_copy(i, d).wait_recv()
        h, span = UNITS[i][0], lanes[i]
        firsts[h, x, :, span] = (part[h, x, :, span] + parts_in[h, 0, :, span]) + (
            parts_in[h, 1, :, span] + parts_in[h, 2, :, span]
        )
        for d in (2, 1, 3):
            start(ag_copy(i, d, x))

    def ag_end(i):
        for d in (1, 3, 2):
            ag_copy(i, d, (x + 4 - d) % 4).wait_recv()

    lane = lax.broadcasted_iota(jnp.int32, (24, 128), 1)

    def first_away(k):
        for t in range(4):
            tile = firsts[k, x, :, pl.ds(t * 128, 128)]
            top, low = tile[:24], tile[24:]
            fold[k, 2 * t] = jnp.where(lane < 64, top, pltpu.roll(low, 64, 1))
            fold[k, 2 * t + 1] = jnp.where(lane < 64, pltpu.roll(top, 64, 1), low)
        for slot in range(8):

            @pl.when(mine[slot])
            def _():
                fold_in[k, zl, x % 2] = fold[k, slot]

            @pl.when(jnp.logical_not(mine[slot]))
            def _():
                remote(
                    fold.at[k, slot], fold_in.at[k, zl, x % 2],
                    fo_send.at[k, slot], fo_recv.at[k, zl, x % 2], device(*taker(slot)),
                ).start()

    def target_of(way, d):
        return (z + (d if way == 0 else 8 - d)) % 8

    def second_early(i):
        k, lo, hi = UNITS[i]
        a = split(firsts[k, :, :, lanes[i]].reshape(192, (hi - lo) * 64))
        for rz in range(4):
            one = product(a, g_tile(k, lo, hi, rz), ((1,), (0,)))
            sums[k, (zl + 4 - rz) % 4] = one.reshape(2, 96, 256)

    def second_late(i, target):
        k, lo, hi = UNITS[i]
        a = split(firsts[k, pl.ds((target // 4) * 2, 2), :, lanes[i]].reshape(96, (hi - lo) * 64))
        b = g_tile(k, lo, hi, (zl + 4 - target % 4) % 4)
        sums[k, target % 4, target // 4] = sums[k, target % 4, target // 4] + product(a, b, ((1,), (0,)))

    def z_copy(k, way, d, j):
        target, rows = target_of(way, d), pl.ds(j * 48, 48)
        return remote(
            sums.at[k, target % 4, target // 4, rows], sums_in.at[k, way, d - 1, rows],
            z_send.at[k, way, d - 1, j], z_recv.at[k, way, d - 1, j], device(x, y, z_step(way), c),
        )

    def z_add(k, way, d, j):
        z_copy(k, way, d, j).wait_recv()
        target, rows = target_of(way, d - 1), pl.ds(j * 48, 48)
        sums[k, target % 4, target // 4, rows] = (
            sums[k, target % 4, target // 4, rows] + sums_in[k, way, d - 1, rows]
        )

    def z_begin(i):
        k = UNITS[i][0]
        second_late(i, target_of(0, 4))
        for way in range(2):
            start(z_copy(k, way, 4, way))
        for way in range(2):
            second_late(i, target_of(way, 3))
            start(z_copy(k, way, 3, 1 - way))
        for d in (2, 1):
            for way in range(2):
                second_late(i, target_of(way, d))
        second_late(i, z)

    def z_round(k, r):
        d = 5 - r
        for turn in range(2):
            for way in range(2):
                j = 1 - way if turn == 0 else way
                if d < 4 or j == way:
                    z_add(k, way, d, j)
                    if d > 1:
                        start(z_copy(k, way, d - 1, j))

    def drain():
        while sent:
            sent.pop().wait_send()

    def first_here(k):
        for which in givers:
            sub, quarter = which
            block = fold_in.at[k, quarter, sub]

            @pl.when(jnp.logical_not(is_me(giver(*which))))
            def _():
                remote(block, block, fo_send.at[0, 0], fo_recv.at[k, quarter, sub], mate).wait_recv()

        for sub in range(2):
            for t in range(2):
                left, right = fold_in[k, 2 * t, sub], fold_in[k, 2 * t + 1, sub]
                rows, span = sub * 48, slice(t * 128, t * 128 + 128)
                first_out[k, rows : rows + 24, span] = jnp.where(lane < 64, left, pltpu.roll(right, 64, 1))
                first_out[k, rows + 24 : rows + 48, span] = jnp.where(lane < 64, pltpu.roll(left, 64, 1), right)

    g_first(0)
    c_start(0, 1)
    g_first(1)
    y_start(0, 1, 0)
    y_start(1, 1, 0)
    y_start(0, 2, 0)
    y_start(1, 2, 0)
    c_start(0, 2)
    y_start(0, 1, 1, 2, 3)
    y_start(0, 3, 0)
    y_start(1, 3, 0)
    c_start(1, 1)
    y_start(1, 1, 1, 2, 3)
    c_start(0, 3)
    y_start(0, 2, 1, 2, 3)
    y_start(0, 4, 0)
    y_start(1, 4, 0)
    y_start(0, 3, 1, 2, 3)
    c_start(0, 4)
    c_start(1, 2)
    y_start(1, 2, 1, 2, 3)
    y_start(0, 4, 1, 2, 3)
    c_start(1, 3)
    y_start(1, 3, 1, 2, 3)
    for way in range(2):
        c_wait(0, way, 4, way)
    first_part(0)
    y_end(0)
    c_start(1, 4)
    y_start(1, 4, 1, 2, 3)
    first_part(1)
    rs_end(0)
    for way in range(2):
        c_wait(1, way, 4, way)
    first_part(2)
    rs_end(1)
    y_end(1)
    first_part(3)
    ag_end(0)
    second_early(0)
    rs_end(2)
    first_away(0)
    ag_end(1)
    z_begin(1)
    rs_end(3)
    z_round(0, 1)
    first_away(1)
    ag_end(2)
    second_early(2)
    ag_end(3)
    z_begin(3)
    z_round(0, 2)
    drain()
    z_round(0, 3)
    z_round(1, 1)
    first_here(0)
    z_round(0, 4)
    second_out[0] = sums[0, zl, zh] * scale[0]
    z_round(1, 2)
    first_here(1)
    drain()
    z_round(1, 3)
    z_round(1, 4)
    second_out[1] = sums[1, zl, zh] * scale[1]
    drain()

    for k in range(2):
        for e, half in pieces:

            @pl.when(jnp.logical_not(is_me(quarter_of(e, half))))
            def _():
                g_copy(k, e, half).wait_send()

        for slot in range(8):

            @pl.when(jnp.logical_not(mine[slot]))
            def _():
                remote(fold.at[k, slot], fold_in.at[0, 0, 0], fo_send.at[k, slot], fo_recv.at[0, 0, 0], mate).wait_send()


def on_device(ci_blocks, integrals, live_counts, walk_kind, walk_sign):
    vmem = pl.BlockSpec(memory_space=pltpu.VMEM)
    dma = pltpu.SemaphoreType.DMA
    shape = jax.ShapeDtypeStruct((2, 96, 256), F32)
    return pl.pallas_call(
        kernel,
        out_shape=(shape, shape),
        in_specs=[pl.BlockSpec(memory_space=pltpu.HBM)] * 5,
        out_specs=(vmem, vmem),
        scratch_shapes=[
            pltpu.VMEM((2, 96, 256), F32),
            pltpu.VMEM((2, 256, 128), F32),
            pltpu.VMEM((1, 1), jnp.int32),
            pltpu.VMEM((1, 96), jnp.int32),
            pltpu.VMEM((1, 96), jnp.int32),
            dma((5,)),
            pltpu.VMEM((2, 128, 256), F32),
            pltpu.VMEM((2, 4, 2, 96, 256), F32),
            pltpu.VMEM((2, 8, 2, 4, 32, 256), F32),
            pltpu.VMEM((2, 4, 48, 512), F32),
            pltpu.VMEM((2, 3, 48, 512), F32),
            pltpu.VMEM((2, 4, 48, 512), F32),
            pltpu.VMEM((2, 8, 24, 128), F32),
            pltpu.VMEM((2, 4, 2, 24, 128), F32),
            pltpu.VMEM((2, 4, 2, 96, 256), F32),
            pltpu.VMEM((2, 2, 4, 96, 256), F32),
            dma((2, 2, 2)), dma((2, 4)),
            dma((2, 2, 4, 2)), dma((2, 2, 4, 2)),
            dma((2, 8)), dma((2, 8)),
            dma((2, 2, 4, 4)), dma((2, 2, 4, 4)),
            dma((4, 3)), dma((4, 3)),
            dma((4, 3)), dma((4, 3)),
            dma((2, 8)), dma((2, 4, 2)),
            dma((2, 2, 4, 2)), dma((2, 2, 4, 2)),
        ],
        compiler_params=pltpu.CompilerParams(
            collective_id=0, has_side_effects=True, vmem_limit_bytes=60 << 20
        ),
        name="sigma",
    )(
        ci_blocks, integrals, live_counts.reshape(1, 1),
        walk_kind.reshape(1, 96), walk_sign.reshape(1, 96),
    )


def solution(mesh):
    placed = (P(None, "walk", "slab"), P(None, "slab", "walk"), P("walk"), P("walk"), P("walk"))
    return jax.shard_map(
        on_device,
        mesh=mesh,
        in_specs=placed,
        out_specs=(P(None, "walk", "slab"), P(None, "walk", "slab")),
        check_vma=False,
    )
```

```python
import functools

import jax
import jax.numpy as jnp
from jax import lax
from jax.experimental import pallas as pl
from jax.experimental.pallas import tpu as pltpu
from jax.sharding import PartitionSpec as P

MESH = pl.DeviceIdType.MESH
F32 = jnp.float32
BF16 = jnp.bfloat16


def device(x, y, z, c):
    return ((z // 4) * 16 + y * 2 + c, x * 4 + z % 4)


def split(a):
    high = a.astype(BF16)
    return high, (a - high.astype(F32)).astype(BF16)


def product(a, b, dims):
    dot = functools.partial(lax.dot_general, dimension_numbers=(dims, ((), ())), preferred_element_type=F32)
    return dot(a[0], b[0]) + (dot(a[0], b[1]) + dot(a[1], b[0]))


OFFSETS = (0, -1, 1, -2, 2, -3, 3, 4)
UNITS = ((0, 0, 6), (0, 6, 8), (1, 0, 6), (1, 6, 8))


def kernel(
    ci_hbm, integrals_hbm, live_hbm, kind_hbm, sign_hbm, first_out, second_out,
    ci, integrals, live, kind, sign, in_sem, turned, cbuf, gbuf, part, parts_in, firsts, fold, fold_in, sums, sums_in,
    g_send, g_recv, c_send, c_recv, m_send, m_recv, y_send, y_recv,
    rs_send, rs_recv, ag_send, ag_recv, fo_send, fo_recv, z_send, z_recv,
):
    loads = [
        pltpu.make_async_copy(src, dst, in_sem.at[i])
        for i, (src, dst) in enumerate(
            zip((integrals_hbm, ci_hbm, live_hbm, kind_hbm, sign_hbm), (integrals, ci, live, kind, sign))
        )
    ]
    for load in loads:
        load.start()
    walk, slab = lax.axis_index("walk"), lax.axis_index("slab")
    x, zl = slab // 4, slab % 4
    zh, y, c = walk // 16, (walk // 2) % 8, walk % 2
    z = zh * 4 + zl

    def remote(src, dst, send, recv, to):
        return pltpu.make_async_remote_copy(
            src_ref=src, dst_ref=dst, send_sem=send, recv_sem=recv, device_id=to, device_id_type=MESH
        )

    givers = [(sub, quarter) for sub in range(2) for quarter in range(4)]

    def giver(sub, quarter):
        return (2 * zh + sub, y, (x // 2) * 4 + quarter, c)

    def is_me(place):
        return (place[0] == x) & (place[1] == y) & (place[2] == z) & (place[3] == c)

    barrier = pltpu.get_barrier_semaphore()
    near = [(x, y, (z + dz) % 8, (c + dc) % 2) for dz in range(8) for dc in range(2) if dz or dc]
    near += [(x, (y + 1) % 8, z, c), (x, (y + 7) % 8, z, c)]
    near += [((x + d) % 4, y, z, c) for d in (1, 2, 3)]
    for place in near:
        pl.semaphore_signal(barrier, inc=1, device_id=device(*place), device_id_type=MESH)
    for which in givers:
        place = giver(*which)

        @pl.when(jnp.logical_not(is_me(place)))
        def _():
            pl.semaphore_signal(barrier, inc=1, device_id=device(*place), device_id_type=MESH)

    def taker(slot):
        yy = (y + OFFSETS[slot] + 8) % 8
        return (2 * zh + yy // 4, y, (x // 2) * 4 + yy % 4, c)

    mine = [is_me(taker(slot)) for slot in range(8)]
    own = functools.reduce(lambda a, b: a + b, [m.astype(jnp.int32) for m in mine])

    rows = lax.broadcasted_iota(jnp.int32, (96, 96), 0)
    cols = lax.broadcasted_iota(jnp.int32, (96, 96), 1)

    def column(line):
        return jnp.sum(jnp.where(rows == cols, jnp.broadcast_to(line, (96, 96)), 0.0), axis=1, keepdims=True)

    for load in loads:
        load.wait()
    position = lax.broadcasted_iota(jnp.int32, (1, 96), 1)
    alive = position < live[...]
    plus = jnp.where(alive & (kind[...] != 1), 1.0, 0.0).astype(F32)
    minus = jnp.where(alive & (kind[...] != 0), 1.0, 0.0).astype(F32) * (2 * sign[...] - 1).astype(F32)
    scale = [column(plus), column(minus)]
    for k in range(2):
        cbuf[k, zl, zh] = ci[k] * scale[k]
        turned[k] = integrals[k].T

    pl.semaphore_wait(barrier, len(near) + 8 - own)

    mate = device(x, y, z, 1 - c)
    sent = []

    def start(copy):
        copy.start()
        sent.append(copy)

    def z_step(way):
        return (z + (1 if way == 0 else 7)) % 8

    def y_step(way):
        return (y + (1 if way == 0 else 7)) % 8

    pieces = [(e, half) for e in range(2) for half in range(2)]

    def quarter_of(e, half):
        return (x, y, zh * 4 + 2 * c + e, half)

    def g_copy(k, e, half):
        return remote(
            turned.at[k, pl.ds(e * 64 + half * 32, 32)], gbuf.at[k, 0, half, (2 * c + e + 4 - zl) % 4],
            g_send.at[k, e, half], g_recv.at[k, (2 * c + e + 4 - zl) % 4], device(*quarter_of(e, half)),
        )

    def g_first(k):
        for e, half in pieces:
            here = is_me(quarter_of(e, half))

            @pl.when(here)
            def _():
                gbuf[k, 0, half, 0] = turned[k, e * 64 + half * 32 : e * 64 + half * 32 + 32]

            @pl.when(jnp.logical_not(here))
            def _():
                g_copy(k, e, half).start()

    def g_wait(k, rz):
        block = gbuf.at[k, 0, c, rz]
        arrived = remote(block, block, g_send.at[k, 0, 0], g_recv.at[k, rz], mate)
        if rz == 0:

            @pl.when(c != zl // 2)
            def _():
                arrived.wait_recv()
        else:
            arrived.wait_recv()

    def c_block(k, way, d, j):
        source = (z + (8 - d if way == 0 else d)) % 8
        return cbuf.at[k, source % 4, source // 4, pl.ds(j * 48, 48)]

    def c_start(k, d):
        for j in range(2):
            for way in range(2):
                if d < 4 or way == j:
                    block = c_block(k, way, d - 1, j)
                    if d > 1:
                        c_wait(k, way, d - 1, j)
                    start(remote(
                        block, block, c_send.at[k, way, d - 1, j], c_recv.at[k, way, d - 1, j],
                        device(x, y, z_step(way), c),
                    ))
                else:
                    c_wait(k, way, d - 1, j)

    def c_wait(k, way, d, j):
        block = c_block(k, way, d, j)
        remote(block, block, c_send.at[k, way, d - 1, j], c_recv.at[k, way, d - 1, j], mate).wait_recv()

    def y_block(k, way, d, rz):
        slot = min(2 * d - 1 + way, 7) if d else 0
        return gbuf.at[k, slot, c, rz]

    def y_wait(k, way, d, rz):
        block = y_block(k, way, d, rz)
        remote(block, block, y_send.at[k, way, d - 1, rz], y_recv.at[k, way, d - 1, rz], mate).wait_recv()

    def y_start(k, d, *chunks):
        for rz in chunks:
            if d == 1:
                g_wait(k, rz)
            for way in range(2):
                if d > 1:
                    y_wait(k, way, d - 1, rz)
                if d < 4 or way == rz // 2:
                    start(remote(
                        y_block(k, way, d - 1, rz), y_block(k, way, d, rz),
                        y_send.at[k, way, d - 1, rz], y_recv.at[k, way, d - 1, rz], device(x, y_step(way), z, c),
                    ))
        if chunks[-1] == 3:
            for slot in (0,) if d == 1 else (2 * d - 3, 2 * d - 2):
                m_start(k, slot)

    def y_end(k):
        for rz in range(4):
            y_wait(k, rz // 2, 4, rz)
        m_start(k, 7)

    def m_start(k, slot):
        block = gbuf.at[k, slot, c]
        start(remote(block, block, m_send.at[k, slot], m_recv.at[k, slot], mate))

    def m_end(k, lo, hi):
        for slot in range(lo, hi):
            block = gbuf.at[k, slot, 1 - c]
            remote(block, block, m_send.at[k, slot], m_recv.at[k, slot], mate).wait_recv()

    lanes = [pl.ds(lo * 64, (hi - lo) * 64) for _, lo, hi in UNITS]

    def g_tile(k, lo, hi, rz):
        return split(gbuf[k, lo:hi, :, rz].reshape((hi - lo) * 64, 256))

    def first_part(i):
        k, lo, hi = UNITS[i]
        m_end(k, lo, hi)
        total = None
        for rz in range(4):
            a = split(cbuf[k, (zl + 4 - rz) % 4].reshape(192, 256))
            one = product(a, g_tile(k, lo, hi, rz), ((1,), (1,)))
            total = one if total is None else total + one
        part[k, :, :, lo * 64 : hi * 64] = total.reshape(4, 48, (hi - lo) * 64)
        for d in (2, 1, 3):
            start(rs_copy(i, d))

    def rs_copy(i, d):
        h = UNITS[i][0]
        return remote(
            part.at[h, (x + d) % 4, :, lanes[i]], parts_in.at[h, d - 1, :, lanes[i]],
            rs_send.at[i, d - 1], rs_recv.at[i, d - 1], device((x + d) % 4, y, z, c),
        )

    def ag_copy(i, d, owner):
        block = firsts.at[UNITS[i][0], owner, :, lanes[i]]
        return remote(block, block, ag_send.at[i, d - 1], ag_recv.at[i, d - 1], device((x + d) % 4, y, z, c))

    def rs_end(i):
        for d in (1, 3, 2):
            rs_copy(i, d).wait_recv()
        h, span = UNITS[i][0], lanes[i]
        firsts[h, x, :, span] = (part[h, x, :, span] + parts_in[h, 0, :, span]) + (
            parts_in[h, 1, :, span] + parts_in[h, 2, :, span]
        )
        for d in (2, 1, 3):
            start(ag_copy(i, d, x))

    def ag_end(i):
        for d in (1, 3, 2):
            ag_copy(i, d, (x + 4 - d) % 4).wait_recv()

    lane = lax.broadcasted_iota(jnp.int32, (24, 128), 1)

    def first_away(k):
        for t in range(4):
            tile = firsts[k, x, :, pl.ds(t * 128, 128)]
            top, low = tile[:24], tile[24:]
            fold[k, 2 * t] = jnp.where(lane < 64, top, pltpu.roll(low, 64, 1))
            fold[k, 2 * t + 1] = jnp.where(lane < 64, pltpu.roll(top, 64, 1), low)
        for slot in range(8):

            @pl.when(mine[slot])
            def _():
                fold_in[k, zl, x % 2] = fold[k, slot]

            @pl.when(jnp.logical_not(mine[slot]))
            def _():
                remote(
                    fold.at[k, slot], fold_in.at[k, zl, x % 2],
                    fo_send.at[k, slot], fo_recv.at[k, zl, x % 2], device(*taker(slot)),
                ).start()

    def target_of(way, d):
        return (z + (d if way == 0 else 8 - d)) % 8

    def second_early(i):
        k, lo, hi = UNITS[i]
        a = split(firsts[k, :, :, lanes[i]].reshape(192, (hi - lo) * 64))
        for rz in range(4):
            one = product(a, g_tile(k, lo, hi, rz), ((1,), (0,)))
            sums[k, (zl + 4 - rz) % 4] = one.reshape(2, 96, 256)

    def second_late(i, target):
        k, lo, hi = UNITS[i]
        a = split(firsts[k, pl.ds((target // 4) * 2, 2), :, lanes[i]].reshape(96, (hi - lo) * 64))
        b = g_tile(k, lo, hi, (zl + 4 - target % 4) % 4)
        sums[k, target % 4, target // 4] = sums[k, target % 4, target // 4] + product(a, b, ((1,), (0,)))

    def z_copy(k, way, d, j):
        target, rows = target_of(way, d), pl.ds(j * 48, 48)
        return remote(
            sums.at[k, target % 4, target // 4, rows], sums_in.at[k, way, d - 1, rows],
            z_send.at[k, way, d - 1, j], z_recv.at[k, way, d - 1, j], device(x, y, z_step(way), c),
        )

    def z_add(k, way, d, j):
        z_copy(k, way, d, j).wait_recv()
        target, rows = target_of(way, d - 1), pl.ds(j * 48, 48)
        sums[k, target % 4, target // 4, rows] = (
            sums[k, target % 4, target // 4, rows] + sums_in[k, way, d - 1, rows]
        )

    def z_begin(i):
        k = UNITS[i][0]
        second_late(i, target_of(0, 4))
        for way in range(2):
            start(z_copy(k, way, 4, way))
        for way in range(2):
            second_late(i, target_of(way, 3))
            start(z_copy(k, way, 3, 1 - way))
        for d in (2, 1):
            for way in range(2):
                second_late(i, target_of(way, d))
        second_late(i, z)

    def z_round(k, r):
        d = 5 - r
        for turn in range(2):
            for way in range(2):
                j = 1 - way if turn == 0 else way
                if d < 4 or j == way:
                    z_add(k, way, d, j)
                    if d > 1:
                        start(z_copy(k, way, d - 1, j))

    def drain():
        while sent:
            sent.pop().wait_send()

    def first_here(k):
        for which in givers:
            sub, quarter = which
            block = fold_in.at[k, quarter, sub]

            @pl.when(jnp.logical_not(is_me(giver(*which))))
            def _():
                remote(block, block, fo_send.at[0, 0], fo_recv.at[k, quarter, sub], mate).wait_recv()

        for sub in range(2):
            for t in range(2):
                left, right = fold_in[k, 2 * t, sub], fold_in[k, 2 * t + 1, sub]
                rows, span = sub * 48, slice(t * 128, t * 128 + 128)
                first_out[k, rows : rows + 24, span] = jnp.where(lane < 64, left, pltpu.roll(right, 64, 1))
                first_out[k, rows + 24 : rows + 48, span] = jnp.where(lane < 64, pltpu.roll(left, 64, 1), right)

    g_first(0)
    c_start(0, 1)
    g_first(1)
    y_start(0, 1, 0)
    y_start(1, 1, 0)
    y_start(0, 2, 0)
    y_start(1, 2, 0)
    c_start(0, 2)
    y_start(0, 1, 1, 2, 3)
    y_start(0, 3, 0)
    y_start(1, 3, 0)
    c_start(1, 1)
    y_start(1, 1, 1, 2, 3)
    c_start(0, 3)
    y_start(0, 2, 1, 2, 3)
    y_start(0, 4, 0)
    y_start(1, 4, 0)
    y_start(0, 3, 1, 2, 3)
    c_start(0, 4)
    c_start(1, 2)
    y_start(1, 2, 1, 2, 3)
    y_start(0, 4, 1, 2, 3)
    c_start(1, 3)
    y_start(1, 3, 1, 2, 3)
    for way in range(2):
        c_wait(0, way, 4, way)
    first_part(0)
    y_end(0)
    c_start(1, 4)
    y_start(1, 4, 1, 2, 3)
    first_part(1)
    rs_end(0)
    for way in range(2):
        c_wait(1, way, 4, way)
    first_part(2)
    rs_end(1)
    y_end(1)
    first_part(3)
    ag_end(0)
    second_early(0)
    rs_end(2)
    first_away(0)
    ag_end(1)
    z_begin(1)
    rs_end(3)
    z_round(0, 1)
    first_away(1)
    ag_end(2)
    second_early(2)
    ag_end(3)
    z_begin(3)
    z_round(1, 1)
    z_round(0, 2)
    z_round(1, 2)
    z_round(0, 3)
    z_round(1, 3)
    first_here(0)
    drain()
    z_round(0, 4)
    second_out[0] = sums[0, zl, zh] * scale[0]
    first_here(1)
    z_round(1, 4)
    second_out[1] = sums[1, zl, zh] * scale[1]
    drain()

    for k in range(2):
        for e, half in pieces:

            @pl.when(jnp.logical_not(is_me(quarter_of(e, half))))
            def _():
                g_copy(k, e, half).wait_send()

        for slot in range(8):

            @pl.when(jnp.logical_not(mine[slot]))
            def _():
                remote(fold.at[k, slot], fold_in.at[0, 0, 0], fo_send.at[k, slot], fo_recv.at[0, 0, 0], mate).wait_send()


def on_device(ci_blocks, integrals, live_counts, walk_kind, walk_sign):
    vmem = pl.BlockSpec(memory_space=pltpu.VMEM)
    dma = pltpu.SemaphoreType.DMA
    shape = jax.ShapeDtypeStruct((2, 96, 256), F32)
    return pl.pallas_call(
        kernel,
        out_shape=(shape, shape),
        in_specs=[pl.BlockSpec(memory_space=pltpu.HBM)] * 5,
        out_specs=(vmem, vmem),
        scratch_shapes=[
            pltpu.VMEM((2, 96, 256), F32),
            pltpu.VMEM((2, 256, 128), F32),
            pltpu.VMEM((1, 1), jnp.int32),
            pltpu.VMEM((1, 96), jnp.int32),
            pltpu.VMEM((1, 96), jnp.int32),
            dma((5,)),
            pltpu.VMEM((2, 128, 256), F32),
            pltpu.VMEM((2, 4, 2, 96, 256), F32),
            pltpu.VMEM((2, 8, 2, 4, 32, 256), F32),
            pltpu.VMEM((2, 4, 48, 512), F32),
            pltpu.VMEM((2, 3, 48, 512), F32),
            pltpu.VMEM((2, 4, 48, 512), F32),
            pltpu.VMEM((2, 8, 24, 128), F32),
            pltpu.VMEM((2, 4, 2, 24, 128), F32),
            pltpu.VMEM((2, 4, 2, 96, 256), F32),
            pltpu.VMEM((2, 2, 4, 96, 256), F32),
            dma((2, 2, 2)), dma((2, 4)),
            dma((2, 2, 4, 2)), dma((2, 2, 4, 2)),
            dma((2, 8)), dma((2, 8)),
            dma((2, 2, 4, 4)), dma((2, 2, 4, 4)),
            dma((4, 3)), dma((4, 3)),
            dma((4, 3)), dma((4, 3)),
            dma((2, 8)), dma((2, 4, 2)),
            dma((2, 2, 4, 2)), dma((2, 2, 4, 2)),
        ],
        compiler_params=pltpu.CompilerParams(
            collective_id=0, has_side_effects=True, vmem_limit_bytes=60 << 20
        ),
        name="sigma",
    )(
        ci_blocks, integrals, live_counts.reshape(1, 1),
        walk_kind.reshape(1, 96), walk_sign.reshape(1, 96),
    )


def solution(mesh):
    placed = (P(None, "walk", "slab"), P(None, "slab", "walk"), P("walk"), P("walk"), P("walk"))
    return jax.shard_map(
        on_device,
        mesh=mesh,
        in_specs=placed,
        out_specs=(P(None, "walk", "slab"), P(None, "walk", "slab")),
        check_vma=False,
    )
```

```python
import functools

import jax
import jax.numpy as jnp
from jax import lax
from jax.experimental import pallas as pl
from jax.experimental.pallas import tpu as pltpu
from jax.sharding import PartitionSpec as P

MESH = pl.DeviceIdType.MESH
F32 = jnp.float32
BF16 = jnp.bfloat16


def device(x, y, z, c):
    return ((z // 4) * 16 + y * 2 + c, x * 4 + z % 4)


def split(a):
    high = a.astype(BF16)
    return high, (a - high.astype(F32)).astype(BF16)


def product(a, b, dims):
    dot = functools.partial(lax.dot_general, dimension_numbers=(dims, ((), ())), preferred_element_type=F32)
    return dot(a[0], b[0]) + (dot(a[0], b[1]) + dot(a[1], b[0]))


OFFSETS = (0, -1, 1, -2, 2, -3, 3, 4)
UNITS = ((0, 0, 6), (0, 6, 8), (1, 0, 6), (1, 6, 8))


def kernel(
    ci_hbm, integrals_hbm, live_hbm, kind_hbm, sign_hbm, first_out, second_out,
    ci, integrals, live, kind, sign, in_sem, turned, cbuf, gbuf, part, parts_in, firsts, fold, fold_in, sums, sums_in,
    g_send, g_recv, c_send, c_recv, m_send, m_recv, y_send, y_recv,
    rs_send, rs_recv, ag_send, ag_recv, fo_send, fo_recv, z_send, z_recv,
):
    loads = [
        pltpu.make_async_copy(src, dst, in_sem.at[i])
        for i, (src, dst) in enumerate(
            zip((integrals_hbm, ci_hbm, live_hbm, kind_hbm, sign_hbm), (integrals, ci, live, kind, sign))
        )
    ]
    for load in loads:
        load.start()
    walk, slab = lax.axis_index("walk"), lax.axis_index("slab")
    x, zl = slab // 4, slab % 4
    zh, y, c = walk // 16, (walk // 2) % 8, walk % 2
    z = zh * 4 + zl

    def remote(src, dst, send, recv, to):
        return pltpu.make_async_remote_copy(
            src_ref=src, dst_ref=dst, send_sem=send, recv_sem=recv, device_id=to, device_id_type=MESH
        )

    givers = [(sub, quarter) for sub in range(2) for quarter in range(4)]

    def giver(sub, quarter):
        return (2 * zh + sub, y, (x // 2) * 4 + quarter, c)

    def is_me(place):
        return (place[0] == x) & (place[1] == y) & (place[2] == z) & (place[3] == c)

    barrier = pltpu.get_barrier_semaphore()
    near = [(x, y, (z + dz) % 8, (c + dc) % 2) for dz in range(8) for dc in range(2) if dz or dc]
    near += [(x, (y + 1) % 8, z, c), (x, (y + 7) % 8, z, c)]
    near += [((x + d) % 4, y, z, c) for d in (1, 2, 3)]
    for place in near:
        pl.semaphore_signal(barrier, inc=1, device_id=device(*place), device_id_type=MESH)
    for which in givers:
        place = giver(*which)

        @pl.when(jnp.logical_not(is_me(place)))
        def _():
            pl.semaphore_signal(barrier, inc=1, device_id=device(*place), device_id_type=MESH)

    def taker(slot):
        yy = (y + OFFSETS[slot] + 8) % 8
        return (2 * zh + yy // 4, y, (x // 2) * 4 + yy % 4, c)

    mine = [is_me(taker(slot)) for slot in range(8)]
    own = functools.reduce(lambda a, b: a + b, [m.astype(jnp.int32) for m in mine])

    rows = lax.broadcasted_iota(jnp.int32, (96, 96), 0)
    cols = lax.broadcasted_iota(jnp.int32, (96, 96), 1)

    def column(line):
        return jnp.sum(jnp.where(rows == cols, jnp.broadcast_to(line, (96, 96)), 0.0), axis=1, keepdims=True)

    for load in loads:
        load.wait()
    position = lax.broadcasted_iota(jnp.int32, (1, 96), 1)
    alive = position < live[...]
    plus = jnp.where(alive & (kind[...] != 1), 1.0, 0.0).astype(F32)
    minus = jnp.where(alive & (kind[...] != 0), 1.0, 0.0).astype(F32) * (2 * sign[...] - 1).astype(F32)
    scale = [column(plus), column(minus)]
    for k in range(2):
        cbuf[k, zl, zh] = ci[k] * scale[k]
        turned[k] = integrals[k].T

    pl.semaphore_wait(barrier, len(near) + 8 - own)

    mate = device(x, y, z, 1 - c)
    sent = []

    def start(copy):
        copy.start()
        sent.append(copy)

    def z_step(way):
        return (z + (1 if way == 0 else 7)) % 8

    def y_step(way):
        return (y + (1 if way == 0 else 7)) % 8

    pieces = [(e, half) for e in range(2) for half in range(2)]

    def quarter_of(e, half):
        return (x, y, zh * 4 + 2 * c + e, half)

    def g_copy(k, e, half):
        return remote(
            turned.at[k, pl.ds(e * 64 + half * 32, 32)], gbuf.at[k, 0, half, (2 * c + e + 4 - zl) % 4],
            g_send.at[k, e, half], g_recv.at[k, (2 * c + e + 4 - zl) % 4], device(*quarter_of(e, half)),
        )

    def g_first(k):
        for e, half in pieces:
            here = is_me(quarter_of(e, half))

            @pl.when(here)
            def _():
                gbuf[k, 0, half, 0] = turned[k, e * 64 + half * 32 : e * 64 + half * 32 + 32]

            @pl.when(jnp.logical_not(here))
            def _():
                g_copy(k, e, half).start()

    def g_wait(k, rz):
        block = gbuf.at[k, 0, c, rz]
        arrived = remote(block, block, g_send.at[k, 0, 0], g_recv.at[k, rz], mate)
        if rz == 0:

            @pl.when(c != zl // 2)
            def _():
                arrived.wait_recv()
        else:
            arrived.wait_recv()

    def c_block(k, way, d, j):
        source = (z + (8 - d if way == 0 else d)) % 8
        return cbuf.at[k, source % 4, source // 4, pl.ds(j * 48, 48)]

    def c_start(k, d):
        for j in range(2):
            for way in range(2):
                if d < 4 or way == j:
                    block = c_block(k, way, d - 1, j)
                    if d > 1:
                        c_wait(k, way, d - 1, j)
                    start(remote(
                        block, block, c_send.at[k, way, d - 1, j], c_recv.at[k, way, d - 1, j],
                        device(x, y, z_step(way), c),
                    ))
                else:
                    c_wait(k, way, d - 1, j)

    def c_wait(k, way, d, j):
        block = c_block(k, way, d, j)
        remote(block, block, c_send.at[k, way, d - 1, j], c_recv.at[k, way, d - 1, j], mate).wait_recv()

    def y_block(k, way, d, rz):
        slot = min(2 * d - 1 + way, 7) if d else 0
        return gbuf.at[k, slot, c, rz]

    def y_wait(k, way, d, rz):
        block = y_block(k, way, d, rz)
        remote(block, block, y_send.at[k, way, d - 1, rz], y_recv.at[k, way, d - 1, rz], mate).wait_recv()

    def y_start(k, d, *chunks):
        for rz in chunks:
            if d == 1:
                g_wait(k, rz)
            for way in range(2):
                if d > 1:
                    y_wait(k, way, d - 1, rz)
                if d < 4 or way == rz // 2:
                    start(remote(
                        y_block(k, way, d - 1, rz), y_block(k, way, d, rz),
                        y_send.at[k, way, d - 1, rz], y_recv.at[k, way, d - 1, rz], device(x, y_step(way), z, c),
                    ))
        if chunks[-1] == 3:
            for slot in (0,) if d == 1 else (2 * d - 3, 2 * d - 2):
                m_start(k, slot)

    def y_end(k):
        for rz in range(4):
            y_wait(k, rz // 2, 4, rz)
        m_start(k, 7)

    def m_start(k, slot):
        block = gbuf.at[k, slot, c]
        start(remote(block, block, m_send.at[k, slot], m_recv.at[k, slot], mate))

    def m_end(k, lo, hi):
        for slot in range(lo, hi):
            block = gbuf.at[k, slot, 1 - c]
            remote(block, block, m_send.at[k, slot], m_recv.at[k, slot], mate).wait_recv()

    lanes = [pl.ds(lo * 64, (hi - lo) * 64) for _, lo, hi in UNITS]

    def g_tile(k, lo, hi, rz):
        return split(gbuf[k, lo:hi, :, rz].reshape((hi - lo) * 64, 256))

    def first_part(i):
        k, lo, hi = UNITS[i]
        m_end(k, lo, hi)
        total = None
        for rz in range(4):
            a = split(cbuf[k, (zl + 4 - rz) % 4].reshape(192, 256))
            one = product(a, g_tile(k, lo, hi, rz), ((1,), (1,)))
            total = one if total is None else total + one
        part[k, :, :, lo * 64 : hi * 64] = total.reshape(4, 48, (hi - lo) * 64)
        for d in (2, 1, 3):
            start(rs_copy(i, d))

    def rs_copy(i, d):
        h = UNITS[i][0]
        return remote(
            part.at[h, (x + d) % 4, :, lanes[i]], parts_in.at[h, d - 1, :, lanes[i]],
            rs_send.at[i, d - 1], rs_recv.at[i, d - 1], device((x + d) % 4, y, z, c),
        )

    def ag_copy(i, d, owner):
        block = firsts.at[UNITS[i][0], owner, :, lanes[i]]
        return remote(block, block, ag_send.at[i, d - 1], ag_recv.at[i, d - 1], device((x + d) % 4, y, z, c))

    def rs_end(i):
        for d in (1, 3, 2):
            rs_copy(i, d).wait_recv()
        h, span = UNITS[i][0], lanes[i]
        firsts[h, x, :, span] = (part[h, x, :, span] + parts_in[h, 0, :, span]) + (
            parts_in[h, 1, :, span] + parts_in[h, 2, :, span]
        )
        for d in (2, 1, 3):
            start(ag_copy(i, d, x))

    def ag_end(i):
        for d in (1, 3, 2):
            ag_copy(i, d, (x + 4 - d) % 4).wait_recv()

    lane = lax.broadcasted_iota(jnp.int32, (24, 128), 1)

    def first_away(k):
        for t in range(4):
            tile = firsts[k, x, :, pl.ds(t * 128, 128)]
            top, low = tile[:24], tile[24:]
            fold[k, 2 * t] = jnp.where(lane < 64, top, pltpu.roll(low, 64, 1))
            fold[k, 2 * t + 1] = jnp.where(lane < 64, pltpu.roll(top, 64, 1), low)
        for slot in range(8):

            @pl.when(mine[slot])
            def _():
                fold_in[k, zl, x % 2] = fold[k, slot]

            @pl.when(jnp.logical_not(mine[slot]))
            def _():
                remote(
                    fold.at[k, slot], fold_in.at[k, zl, x % 2],
                    fo_send.at[k, slot], fo_recv.at[k, zl, x % 2], device(*taker(slot)),
                ).start()

    def target_of(way, d):
        return (z + (d if way == 0 else 8 - d)) % 8

    def second_early(i):
        k, lo, hi = UNITS[i]
        a = split(firsts[k, :, :, lanes[i]].reshape(192, (hi - lo) * 64))
        for rz in range(4):
            one = product(a, g_tile(k, lo, hi, rz), ((1,), (0,)))
            sums[k, (zl + 4 - rz) % 4] = one.reshape(2, 96, 256)

    def second_late(i, target):
        k, lo, hi = UNITS[i]
        a = split(firsts[k, pl.ds((target // 4) * 2, 2), :, lanes[i]].reshape(96, (hi - lo) * 64))
        b = g_tile(k, lo, hi, (zl + 4 - target % 4) % 4)
        sums[k, target % 4, target // 4] = sums[k, target % 4, target // 4] + product(a, b, ((1,), (0,)))

    def z_copy(k, way, d, j):
        target, rows = target_of(way, d), pl.ds(j * 48, 48)
        return remote(
            sums.at[k, target % 4, target // 4, rows], sums_in.at[k, way, d - 1, rows],
            z_send.at[k, way, d - 1, j], z_recv.at[k, way, d - 1, j], device(x, y, z_step(way), c),
        )

    def z_add(k, way, d, j):
        z_copy(k, way, d, j).wait_recv()
        target, rows = target_of(way, d - 1), pl.ds(j * 48, 48)
        sums[k, target % 4, target // 4, rows] = (
            sums[k, target % 4, target // 4, rows] + sums_in[k, way, d - 1, rows]
        )

    def z_begin(i):
        k = UNITS[i][0]
        second_late(i, target_of(0, 4))
        for way in range(2):
            start(z_copy(k, way, 4, way))
        for way in range(2):
            second_late(i, target_of(way, 3))
            start(z_copy(k, way, 3, 1 - way))
        for d in (2, 1):
            for way in range(2):
                second_late(i, target_of(way, d))
        second_late(i, z)

    def z_round(k, r):
        d = 5 - r
        for turn in range(2):
            for way in range(2):
                j = 1 - way if turn == 0 else way
                if d < 4 or j == way:
                    z_add(k, way, d, j)
                    if d > 1:
                        start(z_copy(k, way, d - 1, j))

    def drain():
        while sent:
            sent.pop().wait_send()

    def first_here(k):
        for which in givers:
            sub, quarter = which
            block = fold_in.at[k, quarter, sub]

            @pl.when(jnp.logical_not(is_me(giver(*which))))
            def _():
                remote(block, block, fo_send.at[0, 0], fo_recv.at[k, quarter, sub], mate).wait_recv()

        for sub in range(2):
            for t in range(2):
                left, right = fold_in[k, 2 * t, sub], fold_in[k, 2 * t + 1, sub]
                rows, span = sub * 48, slice(t * 128, t * 128 + 128)
                first_out[k, rows : rows + 24, span] = jnp.where(lane < 64, left, pltpu.roll(right, 64, 1))
                first_out[k, rows + 24 : rows + 48, span] = jnp.where(lane < 64, pltpu.roll(left, 64, 1), right)

    g_first(0)
    c_start(0, 1)
    g_first(1)
    y_start(0, 1, 0)
    y_start(1, 1, 0)
    y_start(0, 2, 0)
    y_start(1, 2, 0)
    c_start(0, 2)
    y_start(0, 1, 1, 2, 3)
    y_start(0, 3, 0)
    y_start(1, 3, 0)
    c_start(1, 1)
    y_start(1, 1, 1, 2, 3)
    c_start(0, 3)
    y_start(0, 2, 1, 2, 3)
    y_start(0, 4, 0)
    y_start(1, 4, 0)
    y_start(0, 3, 1, 2, 3)
    c_start(0, 4)
    c_start(1, 2)
    y_start(1, 2, 1, 2, 3)
    y_start(0, 4, 1, 2, 3)
    c_start(1, 3)
    y_start(1, 3, 1, 2, 3)
    for way in range(2):
        c_wait(0, way, 4, way)
    first_part(0)
    y_end(0)
    c_start(1, 4)
    y_start(1, 4, 1, 2, 3)
    first_part(1)
    rs_end(0)
    for way in range(2):
        c_wait(1, way, 4, way)
    first_part(2)
    rs_end(1)
    y_end(1)
    first_part(3)
    rs_end(2)
    first_away(0)
    ag_end(0)
    second_early(0)
    rs_end(3)
    ag_end(1)
    z_begin(1)
    z_round(0, 1)
    first_away(1)
    ag_end(2)
    second_early(2)
    ag_end(3)
    z_begin(3)
    z_round(1, 1)
    z_round(0, 2)
    z_round(1, 2)
    z_round(0, 3)
    z_round(1, 3)
    first_here(0)
    drain()
    z_round(0, 4)
    second_out[0] = sums[0, zl, zh] * scale[0]
    first_here(1)
    z_round(1, 4)
    second_out[1] = sums[1, zl, zh] * scale[1]
    drain()

    for k in range(2):
        for e, half in pieces:

            @pl.when(jnp.logical_not(is_me(quarter_of(e, half))))
            def _():
                g_copy(k, e, half).wait_send()

        for slot in range(8):

            @pl.when(jnp.logical_not(mine[slot]))
            def _():
                remote(fold.at[k, slot], fold_in.at[0, 0, 0], fo_send.at[k, slot], fo_recv.at[0, 0, 0], mate).wait_send()


def on_device(ci_blocks, integrals, live_counts, walk_kind, walk_sign):
    vmem = pl.BlockSpec(memory_space=pltpu.VMEM)
    dma = pltpu.SemaphoreType.DMA
    shape = jax.ShapeDtypeStruct((2, 96, 256), F32)
    return pl.pallas_call(
        kernel,
        out_shape=(shape, shape),
        in_specs=[pl.BlockSpec(memory_space=pltpu.HBM)] * 5,
        out_specs=(vmem, vmem),
        scratch_shapes=[
            pltpu.VMEM((2, 96, 256), F32),
            pltpu.VMEM((2, 256, 128), F32),
            pltpu.VMEM((1, 1), jnp.int32),
            pltpu.VMEM((1, 96), jnp.int32),
            pltpu.VMEM((1, 96), jnp.int32),
            dma((5,)),
            pltpu.VMEM((2, 128, 256), F32),
            pltpu.VMEM((2, 4, 2, 96, 256), F32),
            pltpu.VMEM((2, 8, 2, 4, 32, 256), F32),
            pltpu.VMEM((2, 4, 48, 512), F32),
            pltpu.VMEM((2, 3, 48, 512), F32),
            pltpu.VMEM((2, 4, 48, 512), F32),
            pltpu.VMEM((2, 8, 24, 128), F32),
            pltpu.VMEM((2, 4, 2, 24, 128), F32),
            pltpu.VMEM((2, 4, 2, 96, 256), F32),
            pltpu.VMEM((2, 2, 4, 96, 256), F32),
            dma((2, 2, 2)), dma((2, 4)),
            dma((2, 2, 4, 2)), dma((2, 2, 4, 2)),
            dma((2, 8)), dma((2, 8)),
            dma((2, 2, 4, 4)), dma((2, 2, 4, 4)),
            dma((4, 3)), dma((4, 3)),
            dma((4, 3)), dma((4, 3)),
            dma((2, 8)), dma((2, 4, 2)),
            dma((2, 2, 4, 2)), dma((2, 2, 4, 2)),
        ],
        compiler_params=pltpu.CompilerParams(
            collective_id=0, has_side_effects=True, vmem_limit_bytes=60 << 20
        ),
        name="sigma",
    )(
        ci_blocks, integrals, live_counts.reshape(1, 1),
        walk_kind.reshape(1, 96), walk_sign.reshape(1, 96),
    )


def solution(mesh):
    placed = (P(None, "walk", "slab"), P(None, "slab", "walk"), P("walk"), P("walk"), P("walk"))
    return jax.shard_map(
        on_device,
        mesh=mesh,
        in_specs=placed,
        out_specs=(P(None, "walk", "slab"), P(None, "walk", "slab")),
        check_vma=False,
    )
```
